128 devices in a mesh: gx: 8 (over y, core), gy: 16 (over z, x).
Axes of the slice: x: 4, y: 4, z: 4, core: 2. Of those that a mesh axis runs over, the one named last changes fastest.
Arguments:
- velocity: float32 [2, 512, 512, 128], P(None, 'gx', 'gy'), may hold values from -6 to 6
- metric: float32 [512, 512, 128], P('gx', 'gy'), may hold values from 0.7 to 1.4
- weights: float32 [262144, 128], P(('gx', 'gy')), may hold values from -0.5 to 0.5
- reynolds: float32 [262144], P(('gx', 'gy')), may hold values from 10 to 300
- face_tile: int32 [262144, 1], P(('gx', 'gy')), may hold values from 0 to 15; in each aligned block of 2048 rows (0 to 2047, 2048 to 4095, ...) at most 256 rows name the same one
- face_cell: int32 [262144], P(('gx', 'gy')), may hold values from 0 to 2047
- profile: float32 [128], replicated, may hold values from 2 to 20
Outputs:
- velocity_out: float32 [2, 512, 512, 128], P(None, 'gx', 'gy')
- stress: float32 [2, 262144], P(None, ('gx', 'gy'))
The draws below stay inside these ranges and needn't reach their ends.
Inputs may be any that keep to these rules, and one draw needn't show every extreme that they name: `face_tile`: among the 2048 faces of one device, at most 256 name the same tile, and in every draw some device has a tile named by exactly 256 of its faces.
All inputs are finite; a program needn't handle non-finite values.
Results may differ from the reference program's by a relative error of at most 0.0001.
Values sent between devices are 32-bit elements; how exact they have to be, the bound alone decides.
A program may use at most 128 MiB of HBM per device.

```python
import math
import jax
import jax.numpy as jnp
import numpy as np
from jax import lax

CX = 64
CY = 32
NZ = 128
F_DEV = 2048
STEPS = 2
WALL_ITERS = 3
CAP = 256
NX = 512
NY = 512
FACES = 262144
N_GY = 16


def plant(drawn, own_key, low, high):
    shape = drawn.shape
    spot = [jax.random.randint(jax.random.fold_in(own_key, axis), (), 0, shape[axis]) for axis in range(len(shape))]
    drawn = drawn.at[tuple(spot)].set(low)
    longest = shape.index(max(shape))
    spot[longest] = (spot[longest] + 1) % shape[longest]
    return drawn.at[tuple(spot)].set(high)


def block_scale(rng, dims, split, least, largest):
    def one(dim, shards_of):
        draws = jax.random.uniform(jax.random.fold_in(jax.random.fold_in(rng, 6), dim), (shards_of,), jnp.float32, least / len(split), largest / len(split))
        return jnp.repeat(jnp.exp(draws), dims[dim] // shards_of).reshape((-1,) + (1,) * (len(dims) - dim - 1))

    factor_of = one(*split[0])
    for cut in split[1:]:
        factor_of = factor_of * one(*cut)
    return factor_of


def shared_out(stream_key, own, number, rows, amount, top, most, slope):
    ranking = jax.random.permutation(stream_key, amount)
    crowded, ordinary = portions_of(amount, rows * top, most, slope, True), portions_of(amount, rows * top, most, slope, False)
    places = jnp.arange(amount)

    def named(sizes, offset_by):
        used = int((sizes > 0).sum())
        fixed = max(1, used // 4)
        moved = fixed + (places - fixed + offset_by * (used - fixed)) % max(1, amount - fixed)
        return jnp.zeros((amount,), jnp.int32).at[ranking[jnp.where(places < fixed, places, moved)]].set(jnp.asarray(sizes, jnp.int32))

    sizes = jnp.where(number % 4 == 0, named(crowded, number // 4), named(ordinary, number - number // 4 - 1))
    mixed = jax.random.permutation(jax.random.fold_in(own, 3), amount)
    giver, receiver = mixed[0:amount // 2 * 2:2], mixed[1:amount // 2 * 2:2]
    slack = jnp.minimum(sizes[giver] - 1, most - sizes[receiver]) // 2
    slack = jnp.where((giver == ranking[0]) | (receiver == ranking[0]) | (sizes[receiver] == 0), 0, jnp.maximum(slack, 0))
    moved = jax.random.randint(jax.random.fold_in(own, 4), (amount // 2,), 0, 1 << 20) % (slack + 1)
    sizes = sizes.at[giver].add(-moved).at[receiver].add(moved)
    members = jnp.searchsorted(jnp.cumsum(sizes), jnp.arange(rows * top), side="right").astype(jnp.int32)
    listing = members.reshape(top, rows).T
    listing = listing[jax.random.permutation(jax.random.fold_in(own, 1), rows)]
    offset_by = jax.random.randint(jax.random.fold_in(own, 2), (rows, 1), 0, top)
    return jnp.take_along_axis(listing, (jnp.arange(top)[None, :] + offset_by) % top, axis=1)


def portions_of(count, total, bound, lean, full):
    weights = [(1 << 20) // math.isqrt(rank ** lean) + 1 for rank in range(1, count + 1)]
    largest = bound if full else min(bound, max(-(-total // count), total * weights[0] // sum(weights)))
    least = 1 if total - largest >= count - 1 else 0
    counts, rest = [largest] + [least] * (count - 1), total - largest - least * (count - 1)
    while rest > 0:
        movable = [i for i in range(1, count) if counts[i] < largest] or [i for i in range(1, count) if counts[i] < bound]
        pool, budget = sum([weights[i] for i in movable]), rest
        for i in movable:
            extra = min(bound - counts[i], max(1, budget * weights[i] // pool), rest)
            counts[i] = counts[i] + extra
            rest = rest - extra
    return np.array(counts)


def scatter_about(key, extent, width, bound, pieces=(), kind=jnp.bfloat16):
    array = jax.random.normal(key, extent, jnp.float32) * width
    if len(pieces) > 0:
        array = block_scale(key, extent, pieces, -0.22, 0.18) * array
    return jnp.clip(array, min=-bound, max=bound).astype(kind)


def setup_inputs(seed: int = 0) -> dict:
    keys = jax.random.split(jax.random.key(seed), 8)
    velocity = scatter_about(keys[0], (2, NX, NY, NZ), 1.0, 6.0, ((1, 8), (2, 16)), jnp.float32)
    metric = jnp.clip(0.7 + 0.7 * jax.random.uniform(keys[1], (NX, NY, NZ), jnp.float32) ** block_scale(keys[1], (NX, NY, NZ), ((0, 8), (1, 16)), -0.2, 0.2), 0.7, 1.4)
    weights = scatter_about(keys[2], (FACES, NZ), NZ ** -0.5, 0.5, ((0, 128),), jnp.float32)
    reynolds = jnp.clip(jnp.exp(math.log(300.0) - 3.4011974 * jax.random.uniform(keys[3], (FACES,), jnp.float32) ** block_scale(keys[3], (FACES,), ((0, 128),), -0.2, 0.2)), 10.0, 300.0)
    face_tile_keys = jax.random.split(jax.random.fold_in(keys[4], 1), FACES // F_DEV)
    face_tile_turns = jax.random.permutation(jax.random.fold_in(keys[4], 3), FACES // F_DEV)
    face_tile = jax.vmap(lambda own, number: shared_out(jax.random.fold_in(keys[4], 2), own, number, F_DEV, N_GY, 1, CAP, 2))(face_tile_keys, face_tile_turns).reshape((FACES, 1))
    face_cell = plant(jax.random.randint(keys[5], (FACES,), 0, CX * CY), jax.random.fold_in(keys[5], 1), 0, (CX * CY) - 1).astype(jnp.int32)
    profile = jnp.clip(jnp.exp(jax.random.uniform(keys[6], (NZ,), jnp.float32, math.log(2.0), math.log(20.0))), 2.0, 20.0)
    return dict(velocity=velocity, metric=metric, weights=weights, reynolds=reynolds, face_tile=face_tile, face_cell=face_cell, profile=profile)


karman = 0.41
time_step = 0.2
viscosity = 0.5

def tendency(widened, metric_wide):
    centre = widened[:, 1:-1, 1:-1]
    east_cell = widened[:, 2:, 1:-1]
    west_cell = widened[:, :-2, 1:-1]
    north_cell = widened[:, 1:-1, 2:]
    south_cell = widened[:, 1:-1, :-2]
    metric_centre = metric_wide[1:-1, 1:-1]
    advect = -0.5 * (centre[0] * (east_cell - west_cell) + centre[1] * (north_cell - south_cell))
    diffuse = 0.5 * (metric_centre + metric_wide[2:, 1:-1]) * (east_cell - centre)
    diffuse = diffuse + 0.5 * (metric_centre + metric_wide[:-2, 1:-1]) * (west_cell - centre)
    diffuse = diffuse + 0.5 * (metric_centre + metric_wide[1:-1, 2:]) * (north_cell - centre)
    diffuse = diffuse + 0.5 * (metric_centre + metric_wide[1:-1, :-2]) * (south_cell - centre)
    zeros_level = jnp.zeros(centre.shape[:-1] + (1,), jnp.float32)
    above = jnp.concatenate([centre[..., 1:], zeros_level], axis=-1)
    below = jnp.concatenate([zeros_level, centre[..., :-1]], axis=-1)
    vertical = (above + below - 2.0 * centre) / (metric_centre * metric_centre)
    return advect + viscosity * (diffuse / metric_centre + vertical)

def wall_stress(matched, reynolds):
    speed_norm = jnp.sqrt(matched[0] * matched[0] + matched[1] * matched[1] + 1.0)
    friction = 0.05 * speed_norm
    for sweep in range(WALL_ITERS):
        friction = karman * speed_norm / jnp.log(9.0 + reynolds * friction)
    return friction * friction * matched / speed_norm

def reference(velocity, metric, weights, reynolds, face_tile, face_cell, profile):
    face_index = jnp.arange(FACES, dtype=jnp.int32)
    row_index = face_index // F_DEV // N_GY
    cell_x = row_index * CX + face_cell // CY
    cell_y = face_tile[:, 0] * CY + face_cell % CY
    metric_wide = jnp.pad(metric, ((1, 1), (1, 1), (0, 0)), mode='wrap')
    stress = jnp.zeros((2, FACES), jnp.float32)
    for step_index in range(STEPS):
        matched_rows = velocity[:, cell_x, cell_y, :]
        matched = lax.optimization_barrier(jnp.sum(matched_rows * weights[None], axis=-1))
        stress = wall_stress(matched, reynolds)
        load = jnp.zeros((2, NX, NY), jnp.float32).at[:, cell_x, cell_y].add(stress)
        widened = jnp.pad(velocity, ((0, 0), (1, 1), (1, 1), (0, 0)), mode='wrap')
        velocity = velocity + time_step * tendency(widened, metric_wide) - load[..., None] * profile
    return (velocity, stress)
```

```python
import jax
import jax.numpy as jnp
from jax import lax
from jax.experimental import pallas as pl
from jax.experimental.pallas import tpu as pltpu
from jax.sharding import PartitionSpec as P

WALL_ITERS = 3
CAP = 256
CX = 64
CY = 32
NZ = 128
FACES = 2048
SIDE = 4
GROUPS = SIDE * SIDE
SLOTS = GROUPS * CAP
CELLS = CX * CY
SPAN = (CX + 2) * CY
HALF = CAP // NZ

karman = 0.41
time_step = 0.2
viscosity = 0.5

MESH = pl.DeviceIdType.MESH
f32 = jnp.float32
bf16 = jnp.bfloat16
i32 = jnp.int32

NT = (((1,), (1,)), ((), ()))


def iota(shape, dim):
    return lax.broadcasted_iota(i32, shape, dim)


def mm(a, b):
    return jnp.dot(a, b, preferred_element_type=f32)


def mm_nt(a, b):
    return lax.dot_general(a, b, NT, preferred_element_type=f32)


def thirds(value):
    first = value.astype(bf16)
    rest = value - first.astype(f32)
    second = rest.astype(bf16)
    third = (rest - second.astype(f32)).astype(bf16)
    return first, second, third


def row_sums(product, ones, diagonal):
    first, second, third = thirds(product)
    total = mm(jnp.concatenate([first, second], axis=1), ones) + mm(third, ones[:NZ])
    rows = []
    for half in range(HALF):
        part = total[half * NZ : (half + 1) * NZ]
        rows.append(jnp.sum(jnp.where(diagonal, part, 0.0), axis=0, keepdims=True))
    return rows


def wall_stress(m0, m1, reynolds):
    speed = jnp.sqrt(m0 * m0 + m1 * m1 + 1.0)
    friction = 0.05 * speed
    for sweep in range(WALL_ITERS):
        friction = karman * speed / jnp.log(9.0 + reynolds * friction)
    factor = friction * friction / speed
    return factor * m0, factor * m1


def kernel(
    vel, met, wgt, rey_ref, tile_ref, cell_ref, prof_ref,
    out, stress_out,
    v0, v1, jac, win, wsend, wrecv, msend, mrecv, mine, lo_face, hi_face, a_face, b_face,
    meta_cell, meta_rey, cell_v, cell_s, inv_v, inv_s, cols, picked, dots, b_slot, a_slot, loads,
    hx, hy, hx2, hy2, ex, ey, ex2, ey2, vout, rsend, rrecv,
    in_sem, smem_sem, ms_sem, mr_sem, ws_sem, wr_sem, hs_sem, hr_sem, rs_sem, rr_sem, out_sem,
):
    gx = lax.axis_index("gx")
    gy = lax.axis_index("gy")
    mz = gy // SIDE
    mx = gy % SIDE

    def peer(step):
        return ((mz + step // SIDE) % SIDE) * SIDE + (mx + step % SIDE) % SIDE

    n_gx = lax.axis_size("gx")
    east = (lax.rem(gx + 1, n_gx), gy)
    west = (lax.rem(gx + n_gx - 1, n_gx), gy)
    north = (gx, lax.rem(gy + 1, GROUPS))
    south = (gx, lax.rem(gy + GROUPS - 1, GROUPS))

    barrier = pltpu.get_barrier_semaphore()
    for step in range(1, GROUPS):
        pl.semaphore_signal(barrier, inc=1, device_id=(gx, peer(step)), device_id_type=MESH)
    for side in (east, west):
        pl.semaphore_signal(barrier, inc=1, device_id=side, device_id_type=MESH)

    loads_in = [
        pltpu.make_async_copy(wgt, win, in_sem.at[0]),
        pltpu.make_async_copy(vel.at[pl.ds(0, CELLS)], v0.at[pl.ds(CY, CELLS)], in_sem.at[1]),
        pltpu.make_async_copy(vel.at[pl.ds(CELLS, CELLS)], v0.at[pl.ds(SPAN + CY, CELLS)], in_sem.at[2]),
        pltpu.make_async_copy(met, jac.at[pl.ds(CY, CELLS)], in_sem.at[3]),
    ]
    for copy in loads_in:
        copy.start()

    chunks = FACES // NZ
    tile = tile_ref[...]
    away = (((tile // SIDE) - mz + SIDE) % SIDE) * SIDE + ((tile % SIDE) - mx + SIDE) % SIDE
    member = jnp.concatenate([(away == t).astype(f32) for t in range(GROUPS)], axis=0)
    member16 = member.astype(bf16)
    upto = (iota((NZ, NZ), 0) <= iota((NZ, NZ), 1)).astype(f32).astype(bf16)
    rows_i = iota((GROUPS * chunks, GROUPS * chunks), 0)
    cols_i = iota((GROUPS * chunks, GROUPS * chunks), 1)
    ahead = ((rows_i // chunks == cols_i // chunks) & (cols_i < rows_i)).astype(f32).astype(bf16)
    ones = jnp.ones((2 * NZ, NZ), bf16)
    earlier = mm(mm(ahead, member16).astype(bf16), ones[:NZ])
    rank = mm(member16, upto) + earlier
    position = jnp.zeros((chunks, NZ), f32)
    for t in range(GROUPS):
        sl = slice(t * chunks, (t + 1) * chunks)
        position = position + member[sl] * (rank[sl] + (t * CAP - 1.0))
    position = position.astype(i32)
    hi = position // NZ
    lo = position % NZ
    hi_face[...] = hi
    lo_face[...] = lo
    cell = cell_ref[...]
    cell_hi = (cell // NZ + 1).astype(f32)
    cell_lo = (cell % NZ).astype(f32)
    r1, r2, r3 = thirds(rey_ref[...])
    r1, r2, r3 = r1.astype(f32), r2.astype(f32), r3.astype(f32)
    lane_row = iota((1, NZ), 1).astype(f32)
    for ch in range(chunks):
        one = slice(ch, ch + 1)
        span = slice(ch * NZ, (ch + 1) * NZ)
        b_face[:, span] = (iota((NZ, NZ), 0) == lo[one]).astype(f32).astype(bf16)
        mask = iota((2 * GROUPS, NZ), 0) == hi[one]
        values = [
            jnp.full((1, NZ), float(ch), f32), lane_row, cell_hi[one], cell_lo[one], r1[one], r2[one], r3[one],
        ]
        a_face[:, span] = jnp.concatenate([jnp.where(mask, v, 0.0) for v in values], axis=0).astype(bf16)
    table = mm_nt(a_face[...], b_face[...])
    part = [table[q * 2 * GROUPS : (q + 1) * 2 * GROUPS] for q in range(7)]
    inv_v[...] = jnp.clip((part[0] * float(NZ) + part[1]).astype(i32), 0, FACES - 1)
    slot_cell = jnp.where(part[2] > 0.0, (part[2] - 1.0) * float(NZ) + part[3], -1.0)
    slot_rey = (part[4] + part[5]) + part[6]
    to_smem = pltpu.make_async_copy(inv_v, inv_s, smem_sem.at[0])
    to_smem.start()
    blank = jnp.zeros((4, NZ), f32)
    for step in range(GROUPS):
        two = slice(step * HALF, (step + 1) * HALF)
        msend[step] = jnp.concatenate([slot_cell[two], slot_rey[two], blank], axis=0)

    pl.semaphore_wait(barrier, GROUPS + 1)

    def meta_copy(step):
        return pltpu.make_async_remote_copy(
            src_ref=msend.at[step], dst_ref=mrecv.at[step],
            send_sem=ms_sem.at[step], recv_sem=mr_sem.at[step],
            device_id=(gx, peer(step)), device_id_type=MESH,
        )

    def weight_copy(step):
        return pltpu.make_async_remote_copy(
            src_ref=wsend.at[pl.ds(step * CAP, CAP)], dst_ref=wrecv.at[pl.ds(step * CAP, CAP)],
            send_sem=ws_sem.at[step], recv_sem=wr_sem.at[step],
            device_id=(gx, peer(step)), device_id_type=MESH,
        )

    def stress_copy(step):
        return pltpu.make_async_remote_copy(
            src_ref=rsend.at[step], dst_ref=rrecv.at[step],
            send_sem=rs_sem.at[step], recv_sem=rr_sem.at[step],
            device_id=(gx, peer(GROUPS - step if step % SIDE == 0 else GROUPS - step + SIDE)),
            device_id_type=MESH,
        )

    for step in range(1, GROUPS):
        meta_copy(step).start()

    to_smem.wait()
    loads_in[0].wait()

    def pack(step):
        def some(g, carry):
            for u in range(16):
                slot = g * 16 + u
                face = inv_s[step * HALF + g // 8, (g % 8) * 16 + u]
                wsend[pl.ds(step * CAP + slot, 1), :] = win[pl.ds(face, 1), :]
            return carry

        lax.fori_loop(0, CAP // 16, some, 0)

    def pack_send(step, carry):
        pack(step)
        weight_copy(step).start()
        return carry

    lax.fori_loop(1, GROUPS, pack_send, 0)
    pack(0)

    for copy in loads_in[1:]:
        copy.wait()

    def edges(buffer, jacobian, x_edge, y_edge):
        for n, at in enumerate((CY, CX * CY)):
            for c in range(2):
                x_edge[n, pl.ds(c * CY, CY), :] = buffer[pl.ds(c * SPAN + at, CY), :]
            if jacobian is not None:
                x_edge[n, pl.ds(2 * CY, CY), :] = jacobian[pl.ds(at, CY), :]
        for n, at in enumerate((CY, CY + CY - 1)):
            for c in range(2):
                y_edge[n, pl.ds(c * CX, CX), :] = buffer[pl.ds(c * SPAN + at, CX, stride=CY), :]
            if jacobian is not None:
                y_edge[n, pl.ds(2 * CX, CX), :] = jacobian[pl.ds(at, CX, stride=CY), :]

    def halo_copies(x_edge, y_edge, x_halo, y_halo, base):
        made = []
        for n, (edge, halo, way, device) in enumerate((
            (x_edge, x_halo, 0, west), (x_edge, x_halo, 1, east),
            (y_edge, y_halo, 0, south), (y_edge, y_halo, 1, north),
        )):
            made.append(pltpu.make_async_remote_copy(
                src_ref=edge.at[way], dst_ref=halo.at[way],
                send_sem=hs_sem.at[base + n], recv_sem=hr_sem.at[base + n],
                device_id=device, device_id_type=MESH,
            ))
        return made

    edges(v0, jac, ex, ey)
    halos = halo_copies(ex, ey, hx, hy, 0)
    for copy in halos:
        copy.start()

    mine[...] = msend[0]
    for step in range(GROUPS):
        two = slice(step * HALF, (step + 1) * HALF)
        if step:
            meta_copy(step).wait_recv()
            block = mrecv[step]
        else:
            block = mine[...]
        meta_cell[two, :] = block[0:HALF]
        meta_rey[two, :] = block[HALF : 2 * HALF]
    slot_of = meta_cell[...].astype(i32)
    cell_v[...] = jnp.clip(slot_of, 0, CELLS - 1) * 4
    cells_smem = pltpu.make_async_copy(cell_v, cell_s, smem_sem.at[1])
    cells_smem.start()
    used = slot_of >= 0
    s_hi = jnp.where(used, slot_of // NZ, -1)
    s_lo = jnp.where(used, slot_of % NZ, -1)
    for j in range(2 * GROUPS):
        b_slot[:, j * NZ : (j + 1) * NZ] = (iota((NZ, NZ), 0) == s_lo[j : j + 1]).astype(f32).astype(bf16)

    for copy in halos:
        copy.wait_recv()

    row_y = iota((CY, NZ), 0)
    lane = iota((CY, NZ), 1)
    at_first, at_last = row_y == 0, row_y == CY - 1
    top, bottom = lane == NZ - 1, lane == 0

    for c in range(2):
        v0[pl.ds(c * SPAN + (CX + 1) * CY, CY), :] = hx[0, pl.ds(c * CY, CY), :]
        v0[pl.ds(c * SPAN, CY), :] = hx[1, pl.ds(c * CY, CY), :]
    jac[pl.ds((CX + 1) * CY, CY), :] = hx[0, pl.ds(2 * CY, CY), :]
    jac[pl.ds(0, CY), :] = hx[1, pl.ds(2 * CY, CY), :]

    def star(buffer, base, halo, row, x):
        at = pl.multiple_of(base + (x + 1) * CY, CY)
        centre = buffer[pl.ds(at, CY), :]
        next_x = buffer[pl.ds(pl.multiple_of(at + CY, CY), CY), :]
        last_x = buffer[pl.ds(pl.multiple_of(at - CY, CY), CY), :]
        next_y = pltpu.roll(centre, CY - 1, 0)
        last_y = pltpu.roll(centre, 1, 0)
        next_y = jnp.where(at_last, halo[0, pl.ds(row + x, 1), :], next_y)
        last_y = jnp.where(at_first, halo[1, pl.ds(row + x, 1), :], last_y)
        return centre, next_x, last_x, next_y, last_y

    def advance(buffer, halo, x):
        j, j_e, j_w, j_n, j_s = star(jac, 0, hy, 2 * CX, x)
        inverse = 1.0 / j
        k_e, k_w, k_n, k_s = j + j_e, j + j_w, j + j_n, j + j_s
        k_h = (time_step * viscosity * 0.5) * inverse
        k_v = (time_step * viscosity) * inverse * inverse
        stars = [star(buffer, c * SPAN, halo, c * CX, x) for c in range(2)]
        along = (-0.5 * time_step) * stars[0][0]
        across = (-0.5 * time_step) * stars[1][0]
        results = []
        for c in range(2):
            v, e, w, n, s = stars[c]
            spread = k_e * (e - v) + k_w * (w - v) + k_n * (n - v) + k_s * (s - v)
            above = jnp.where(top, 0.0, pltpu.roll(v, NZ - 1, 1))
            below = jnp.where(bottom, 0.0, pltpu.roll(v, 1, 1))
            change = along * (e - w) + across * (n - s) + k_h * spread + k_v * (above + below - 2.0 * v)
            results.append((v, change))
        return results

    def first_step(x, carry):
        for c, (v, change) in enumerate(advance(v0, hy, x)):
            new = v + change
            v1[pl.ds(pl.multiple_of(c * SPAN + (x + 1) * CY, CY), CY), :] = new
            cols[pl.ds(x * (4 * CY) + c, CY, stride=4), :] = v
            cols[pl.ds(x * (4 * CY) + 2 + c, CY, stride=4), :] = new
        return carry

    lax.fori_loop(0, CX, first_step, 0)

    cells_smem.wait()
    diagonal = iota((NZ, NZ), 0) == iota((NZ, NZ), 1)
    profile = prof_ref[...]

    def chunk(step, source):
        def some(g, carry):
            for u in range(16):
                slot = g * 16 + u
                where = cell_s[step * HALF + g // 8, (g % 8) * 16 + u]
                picked[pl.ds(slot * 4, 4), :] = cols[pl.ds(where, 4), :]
            return carry

        lax.fori_loop(0, CAP // 16, some, 0)
        weights = source[pl.ds(pl.multiple_of(step * CAP, CAP), CAP), :]
        for q in range(5):
            if q < 4:
                product = picked[pl.ds(q, CAP, stride=4), :] * weights
            else:
                product = weights * profile
            for half, row in enumerate(row_sums(product, ones, diagonal)):
                dots[q, pl.ds(step * HALF + half, 1), :] = row

    chunk(0, wsend)

    def arrived(step, carry):
        weight_copy(step).wait_recv()
        chunk(step, wrecv)
        return carry

    lax.fori_loop(1, GROUPS, arrived, 0)

    reynolds = meta_rey[...]

    def load_of(stress):
        pieces = [thirds(jnp.where(used, s, 0.0)) for s in stress]
        pieces = [[p.astype(f32) for p in piece] for piece in pieces]
        for j in range(2 * GROUPS):
            one = slice(j, j + 1)
            mask = iota((GROUPS, NZ), 0) == s_hi[one]
            parts = [jnp.where(mask, pieces[c][k][one], 0.0) for k in range(3) for c in range(2)]
            parts.append(jnp.zeros((2 * GROUPS, NZ), f32))
            a_slot[:, j * NZ : (j + 1) * NZ] = jnp.concatenate(parts, axis=0).astype(bf16)
        total = mm_nt(b_slot[...], a_slot[...])
        return total + pltpu.roll(total, NZ - 2 * GROUPS, 1) + pltpu.roll(total, NZ - 4 * GROUPS, 1)

    stress = wall_stress(dots[0], dots[1], reynolds)
    load = load_of(stress)
    for c in range(2):
        for block in range(CELLS // NZ):
            at = pl.ds(c * SPAN + CY + block * NZ, NZ)
            column = c * GROUPS + block
            v1[at, :] = v1[at, :] - load[:, column : column + 1] * profile

    edges(v1, None, ex2, ey2)
    halos2 = halo_copies(ex2, ey2, hx2, hy2, 4)
    for copy in halos2:
        copy.start()

    by_column = jnp.transpose(load)[0 : 2 * GROUPS]
    pieces = thirds(by_column)
    for j in range(2 * GROUPS):
        seen = b_slot[:, j * NZ : (j + 1) * NZ]
        spread = mm(pieces[0], seen) + mm(pieces[1], seen) + mm(pieces[2], seen)
        mask = iota((GROUPS, NZ), 0) == s_hi[j : j + 1]
        for c in range(2):
            at_face = jnp.where(mask, spread[c * GROUPS : (c + 1) * GROUPS], 0.0)
            loads[c, j : j + 1, :] = jnp.sum(at_face, axis=0, keepdims=True)
    stress = wall_stress(dots[2] - loads[0] * dots[4], dots[3] - loads[1] * dots[4], reynolds)
    for step in range(GROUPS):
        two = slice(step * HALF, (step + 1) * HALF)
        rsend[step] = jnp.concatenate([stress[0][two], stress[1][two], blank], axis=0)
    for step in range(1, GROUPS):
        stress_copy(step).start()

    load = load_of(stress)
    for c in range(2):
        for block in range(CELLS // NZ):
            at = pl.ds(c * SPAN + CY + block * NZ, NZ)
            column = c * GROUPS + block
            vout[pl.ds(c * CELLS + block * NZ, NZ), :] = v1[at, :] - load[:, column : column + 1] * profile

    for copy in halos2:
        copy.wait_recv()
    for c in range(2):
        v1[pl.ds(c * SPAN + (CX + 1) * CY, CY), :] = hx2[0, pl.ds(c * CY, CY), :]
        v1[pl.ds(c * SPAN, CY), :] = hx2[1, pl.ds(c * CY, CY), :]

    quarter = CX // 4
    stores = []
    for k in range(4):
        def second_step(x, carry):
            for c, (v, change) in enumerate(advance(v1, hy2, x)):
                at = pl.ds(pl.multiple_of(c * CELLS + x * CY, CY), CY)
                vout[at, :] = vout[at, :] + change
            return carry

        lax.fori_loop(k * quarter, (k + 1) * quarter, second_step, 0)
        for c in range(2):
            at = pl.ds(c * CELLS + k * quarter * CY, quarter * CY)
            copy = pltpu.make_async_copy(vout.at[at], out.at[at], out_sem.at[2 * k + c])
            copy.start()
            stores.append(copy)

    mine[...] = rsend[0]
    for step in range(1, GROUPS):
        stress_copy(step).wait_recv()
    back = jnp.concatenate([mine[...]] + [rrecv[step] for step in range(1, GROUPS)], axis=0)
    pieces = thirds(back)
    for ch in range(chunks):
        one = slice(ch, ch + 1)
        span = slice(ch * NZ, (ch + 1) * NZ)
        seen = b_face[:, span]
        spread = mm(pieces[0], seen) + mm(pieces[1], seen) + mm(pieces[2], seen)
        place = hi_face[one, :]
        row = (place // HALF) * 8 + place % HALF
        for c in range(2):
            mask = iota((8 * GROUPS, NZ), 0) == row + c * HALF
            stress_out[c : c + 1, span] = jnp.sum(jnp.where(mask, spread, 0.0), axis=0, keepdims=True)

    for copy in stores:
        copy.wait()
    for copy in halos + halos2:
        copy.wait_send()
    for step in range(1, GROUPS):
        meta_copy(step).wait_send()
        weight_copy(step).wait_send()
        stress_copy(step).wait_send()


def local(velocity, metric, weights, reynolds, face_tile, face_cell, profile):
    vm = pltpu.VMEM
    dma = pltpu.SemaphoreType.DMA
    small = (FACES // NZ, NZ)
    scratch = [
        vm((2 * SPAN, NZ), f32), vm((2 * SPAN, NZ), f32), vm((SPAN, NZ), f32), vm((FACES, NZ), f32),
        vm((SLOTS, NZ), f32), vm((SLOTS, NZ), f32),
        vm((GROUPS, 8, NZ), f32), vm((GROUPS, 8, NZ), f32), vm((8, NZ), f32),
        vm(small, i32), vm(small, i32), vm((14 * GROUPS, FACES), bf16), vm((NZ, FACES), bf16),
        vm((2 * GROUPS, NZ), f32), vm((2 * GROUPS, NZ), f32),
        vm((2 * GROUPS, NZ), i32), pltpu.SMEM((2 * GROUPS, NZ), i32),
        vm((2 * GROUPS, NZ), i32), pltpu.SMEM((2 * GROUPS, NZ), i32),
        vm((4 * CELLS + 8, NZ), f32), vm((4 * CAP + 8, NZ), f32), vm((5, 2 * GROUPS, NZ), f32),
        vm((NZ, SLOTS), bf16), vm((NZ, SLOTS), bf16), vm((2, 2 * GROUPS, NZ), f32),
        vm((2, 3 * CY, NZ), f32), vm((2, 3 * CX, NZ), f32), vm((2, 2 * CY, NZ), f32), vm((2, 2 * CX, NZ), f32),
        vm((2, 3 * CY, NZ), f32), vm((2, 3 * CX, NZ), f32), vm((2, 2 * CY, NZ), f32), vm((2, 2 * CX, NZ), f32),
        vm((2 * CELLS, NZ), f32), vm((GROUPS, 8, NZ), f32), vm((GROUPS, 8, NZ), f32),
        dma((4,)), dma((2,)), dma((GROUPS,)), dma((GROUPS,)), dma((GROUPS,)), dma((GROUPS,)),
        dma((8,)), dma((8,)), dma((GROUPS,)), dma((GROUPS,)), dma((8,)),
    ]
    whole = pl.BlockSpec(memory_space=pl.ANY)
    inside = pl.BlockSpec(memory_space=pltpu.VMEM)
    out, stress = pl.pallas_call(
        kernel,
        out_shape=(
            jax.ShapeDtypeStruct((2 * CELLS, NZ), f32),
            jax.ShapeDtypeStruct((2, FACES), f32),
        ),
        in_specs=[whole, whole, whole, inside, inside, inside, inside],
        out_specs=(whole, inside),
        scratch_shapes=scratch,
        compiler_params=pltpu.CompilerParams(
            collective_id=0, has_side_effects=True, vmem_limit_bytes=48 * 1024 * 1024
        ),
    )(
        velocity.reshape(2 * CELLS, NZ), metric.reshape(CELLS, NZ), weights,
        reynolds.reshape(small), face_tile.reshape(small), face_cell.reshape(small), profile.reshape(1, NZ),
    )
    return out.reshape(2, CX, CY, NZ), stress


def solution(mesh):
    placed = (
        P(None, "gx", "gy", None),
        P("gx", "gy", None),
        P(("gx", "gy"), None),
        P(("gx", "gy")),
        P(("gx", "gy"), None),
        P(("gx", "gy")),
        P(),
    )
    return jax.shard_map(
        local,
        mesh=mesh,
        in_specs=placed,
        out_specs=(P(None, "gx", "gy", None), P(None, ("gx", "gy"))),
        check_vma=False,
    )
```

```python
import jax
import jax.numpy as jnp
from jax import lax
from jax.experimental import pallas as pl
from jax.experimental.pallas import tpu as pltpu
from jax.sharding import PartitionSpec as P

WALL_ITERS = 3
CAP = 256
CX = 64
CY = 32
NZ = 128
FACES = 2048
SIDE = 4
GROUPS = SIDE * SIDE
SLOTS = GROUPS * CAP
CELLS = CX * CY
SPAN = (CX + 2) * CY
BLOCK = CAP // 8

karman = 0.41
time_step = 0.2
viscosity = 0.5

MESH = pl.DeviceIdType.MESH
f32 = jnp.float32
bf16 = jnp.bfloat16
i32 = jnp.int32

NT = (((1,), (1,)), ((), ()))

ORDER = (4, 12, 1, 3, 8, 2, 5, 15, 7, 13, 10, 6, 14, 9, 11)


def iota(shape, dim):
    return lax.broadcasted_iota(i32, shape, dim)


def mm(a, b):
    return jnp.dot(a, b, preferred_element_type=f32)


def mm_nt(a, b):
    return lax.dot_general(a, b, NT, preferred_element_type=f32)


def thirds(value):
    first = value.astype(bf16)
    rest = value - first.astype(f32)
    second = rest.astype(bf16)
    third = (rest - second.astype(f32)).astype(bf16)
    return first, second, third


def fold(values, level):
    n = values.shape[0]
    gap = 1 << level
    pair = values.reshape(n // 2, 2, 8, NZ)
    first, second = pair[:, 0], pair[:, 1]
    low = (iota((n // 2, 8, NZ), 2) & gap) == 0
    kept = jnp.where(low, first, second)
    moved = jnp.where(low, second, first).reshape(n * 4, NZ)
    return kept + pltpu.roll(moved, NZ - gap, 1).reshape(n // 2, 8, NZ)


def nth(index):
    words = [sum(step << (4 * k) for k, step in enumerate(ORDER[h : h + 7])) for h in (0, 7, 14)]
    word = jnp.where(index < 7, words[0], jnp.where(index < 14, words[1], words[2]))
    return (word >> (4 * (index % 7))) & 15


def wall_stress(m0, m1, reynolds):
    speed = jnp.sqrt(m0 * m0 + m1 * m1 + 1.0)
    friction = 0.05 * speed
    for sweep in range(WALL_ITERS):
        friction = karman * speed / jnp.log(9.0 + reynolds * friction)
    factor = friction * friction / speed
    return factor * m0, factor * m1


def kernel(
    vel, met, wgt, rey_in, tile_in, cell_in, prof_in,
    out, stress_out,
    v0, v1, jac, win, wsend, wrecv, msend, mrecv, lo_face, hi_face, a_face, b_face,
    meta_cell, meta_rey, cell_v, cell_s, inv_v, inv_s, cols, picked, dots, b_slot, a_slot, loads,
    hx, hy, hx2, hy2, ex, ey, ex2, ey2, rsend, rrecv,
    rey_ref, tile_ref, cell_ref, prof_ref,
    in_sem, smem_sem, ms_sem, mr_sem, ws_sem, wr_sem, hs_sem, hr_sem, rs_sem, rr_sem,
):
    gx = lax.axis_index("gx")
    gy = lax.axis_index("gy")
    mz = gy // SIDE
    mx = gy % SIDE

    def peer(step):
        return ((mz + step // SIDE) % SIDE) * SIDE + (mx + step % SIDE) % SIDE

    n_gx = lax.axis_size("gx")
    east = (lax.rem(gx + 1, n_gx), gy)
    west = (lax.rem(gx + n_gx - 1, n_gx), gy)
    north = (gx, lax.rem(gy + 1, GROUPS))
    south = (gx, lax.rem(gy + GROUPS - 1, GROUPS))

    barrier = pltpu.get_barrier_semaphore()
    for step in range(1, GROUPS):
        pl.semaphore_signal(barrier, inc=1, device_id=(gx, peer(step)), device_id_type=MESH)
    for side in (east, west):
        pl.semaphore_signal(barrier, inc=1, device_id=side, device_id_type=MESH)

    small_in = [
        pltpu.make_async_copy(tile_in, tile_ref, in_sem.at[4]),
        pltpu.make_async_copy(cell_in, cell_ref, in_sem.at[5]),
        pltpu.make_async_copy(rey_in, rey_ref, in_sem.at[6]),
        pltpu.make_async_copy(prof_in, prof_ref, in_sem.at[7]),
    ]
    for copy in small_in:
        copy.start()
    loads_in = [
        pltpu.make_async_copy(wgt, win, in_sem.at[0]),
        pltpu.make_async_copy(vel.at[pl.ds(0, CELLS)], v0.at[pl.ds(CY, CELLS)], in_sem.at[1]),
        pltpu.make_async_copy(vel.at[pl.ds(CELLS, CELLS)], v0.at[pl.ds(SPAN + CY, CELLS)], in_sem.at[2]),
        pltpu.make_async_copy(met, jac.at[pl.ds(CY, CELLS)], in_sem.at[3]),
    ]
    for copy in loads_in:
        copy.start()

    for copy in small_in:
        copy.wait()
    chunks = FACES // NZ
    tile = tile_ref[...]
    away = (((tile // SIDE) - mz + SIDE) % SIDE) * SIDE + ((tile % SIDE) - mx + SIDE) % SIDE
    member = jnp.concatenate([(away == t).astype(f32) for t in range(GROUPS)], axis=0)
    member16 = member.astype(bf16)
    upto = (iota((NZ, NZ), 0) <= iota((NZ, NZ), 1)).astype(f32).astype(bf16)
    rows_i = iota((GROUPS * chunks, GROUPS * chunks), 0)
    cols_i = iota((GROUPS * chunks, GROUPS * chunks), 1)
    ahead = ((rows_i // chunks == cols_i // chunks) & (cols_i < rows_i)).astype(f32).astype(bf16)
    ones = jnp.ones((2 * NZ, NZ), bf16)
    earlier = mm(mm(ahead, member16).astype(bf16), ones[:NZ])
    rank = mm(member16, upto) + earlier
    order = jnp.zeros((chunks, NZ), f32)
    for t in range(GROUPS):
        sl = slice(t * chunks, (t + 1) * chunks)
        order = order + member[sl] * rank[sl]
    order = order.astype(i32) - 1
    hi = (away // SIDE) * 8 + order % 8
    lo = (away % SIDE) * BLOCK + order // 8
    hi_face[...] = hi
    lo_face[...] = lo
    cell = cell_ref[...]
    cell_hi = (cell // NZ + 1).astype(f32)
    cell_lo = (cell % NZ).astype(f32)
    r1, r2, r3 = thirds(rey_ref[...])
    r1, r2, r3 = r1.astype(f32), r2.astype(f32), r3.astype(f32)
    lane_row = iota((1, NZ), 1).astype(f32)
    for ch in range(chunks):
        one = slice(ch, ch + 1)
        span = slice(ch * NZ, (ch + 1) * NZ)
        b_face[:, span] = (iota((NZ, NZ), 0) == lo[one]).astype(f32).astype(bf16)
        mask = iota((2 * GROUPS, NZ), 0) == hi[one]
        values = [
            jnp.full((1, NZ), float(ch), f32), lane_row, cell_hi[one], cell_lo[one], r1[one], r2[one], r3[one],
        ]
        a_face[:, span] = jnp.concatenate([jnp.where(mask, v, 0.0) for v in values], axis=0).astype(bf16)
    table = mm_nt(a_face[...], b_face[...])
    part = [table[q * 2 * GROUPS : (q + 1) * 2 * GROUPS] for q in range(7)]
    inv_v[...] = jnp.clip((part[0] * float(NZ) + part[1]).astype(i32), 0, FACES - 1)
    slot_cell = jnp.where(part[2] > 0.0, (part[2] - 1.0) * float(NZ) + part[3], -1.0)
    slot_rey = (part[4] + part[5]) + part[6]
    to_smem = pltpu.make_async_copy(inv_v, inv_s, smem_sem.at[0])
    to_smem.start()
    for g in range(SIDE):
        eight = slice(g * 8, (g + 1) * 8)
        msend[g] = jnp.concatenate([slot_cell[eight], slot_rey[eight]], axis=0)

    def meta_copy(step):
        return pltpu.make_async_remote_copy(
            src_ref=msend.at[step // SIDE], dst_ref=mrecv.at[step],
            send_sem=ms_sem.at[step], recv_sem=mr_sem.at[step],
            device_id=(gx, peer(step)), device_id_type=MESH,
        )

    def weight_copy(step):
        return pltpu.make_async_remote_copy(
            src_ref=wsend.at[pl.ds(step * CAP, CAP)], dst_ref=wrecv.at[pl.ds(step * CAP, CAP)],
            send_sem=ws_sem.at[step], recv_sem=wr_sem.at[step],
            device_id=(gx, peer(step)), device_id_type=MESH,
        )

    def stress_copy(step):
        return pltpu.make_async_remote_copy(
            src_ref=rsend.at[step // SIDE], dst_ref=rrecv.at[step],
            send_sem=rs_sem.at[step], recv_sem=rr_sem.at[step],
            device_id=(gx, peer(GROUPS - step if step % SIDE == 0 else GROUPS - step + SIDE)),
            device_id_type=MESH,
        )

    def pack(step):
        def some(g, carry):
            rows = []
            for u in range(16):
                face = inv_s[(step // SIDE) * 8 + u % 8, (step % SIDE) * BLOCK + g * 2 + u // 8]
                rows.append(win[pl.ds(face, 1), :])
            for u in range(16):
                wsend[pl.ds(step * CAP + g * 16 + u, 1), :] = rows[u]
            return carry

        lax.fori_loop(0, CAP // 16, some, 0)

    def pack_send(index, carry):
        step = nth(index)
        pack(step)
        weight_copy(step).start()
        return carry

    to_smem.wait()
    loads_in[0].wait()
    pack(ORDER[0])

    pl.semaphore_wait(barrier, GROUPS + 1)
    for step in ORDER:
        meta_copy(step).start()
    weight_copy(ORDER[0]).start()
    lax.fori_loop(1, 4, pack_send, 0)

    for copy in loads_in[1:]:
        copy.wait()

    def edges(buffer, jacobian, x_edge, y_edge):
        for n, at in enumerate((CY, CX * CY)):
            for c in range(2):
                x_edge[n, pl.ds(c * CY, CY), :] = buffer[pl.ds(c * SPAN + at, CY), :]
            if jacobian is not None:
                x_edge[n, pl.ds(2 * CY, CY), :] = jacobian[pl.ds(at, CY), :]
        for n, at in enumerate((CY, CY + CY - 1)):
            for c in range(2):
                y_edge[n, pl.ds(c * CX, CX), :] = buffer[pl.ds(c * SPAN + at, CX, stride=CY), :]
            if jacobian is not None:
                y_edge[n, pl.ds(2 * CX, CX), :] = jacobian[pl.ds(at, CX, stride=CY), :]

    def halo_copies(x_edge, y_edge, x_halo, y_halo, base):
        made = []
        for n, (edge, halo, way, device) in enumerate((
            (x_edge, x_halo, 0, west), (x_edge, x_halo, 1, east),
            (y_edge, y_halo, 0, south), (y_edge, y_halo, 1, north),
        )):
            made.append(pltpu.make_async_remote_copy(
                src_ref=edge.at[way], dst_ref=halo.at[way],
                send_sem=hs_sem.at[base + n], recv_sem=hr_sem.at[base + n],
                device_id=device, device_id_type=MESH,
            ))
        return made

    edges(v0, jac, ex, ey)
    halos = halo_copies(ex, ey, hx, hy, 0)
    for copy in halos:
        copy.start()

    lax.fori_loop(4, GROUPS - 1, pack_send, 0)
    pack(0)

    for step in range(1, GROUPS):
        meta_copy(step).wait_recv()
    lanes16 = iota((16, NZ), 1) // BLOCK

    def four(first, received, g):
        rows = first if g == 0 else received[g * SIDE]
        for k in range(1, SIDE):
            rows = jnp.where(lanes16 == k, received[g * SIDE + k], rows)
        return rows

    for g in range(SIDE):
        rows = four(msend[0], mrecv, g)
        meta_cell[g * 8 : (g + 1) * 8, :] = rows[0:8]
        meta_rey[g * 8 : (g + 1) * 8, :] = rows[8:16]
    slot_of = meta_cell[...].astype(i32)
    cell_v[...] = jnp.clip(slot_of, 0, CELLS - 1) * 4
    cells_smem = pltpu.make_async_copy(cell_v, cell_s, smem_sem.at[1])
    cells_smem.start()
    used = slot_of >= 0
    s_hi = jnp.where(used, slot_of // NZ, -1)
    s_lo = jnp.where(used, slot_of % NZ, -1)
    for j in range(2 * GROUPS):
        b_slot[:, j * NZ : (j + 1) * NZ] = (iota((NZ, NZ), 0) == s_lo[j : j + 1]).astype(f32).astype(bf16)

    for copy in halos:
        copy.wait_recv()

    row_y = iota((CY, NZ), 0)
    lane = iota((CY, NZ), 1)
    at_first, at_last = row_y == 0, row_y == CY - 1
    top, bottom = lane == NZ - 1, lane == 0

    for c in range(2):
        v0[pl.ds(c * SPAN + (CX + 1) * CY, CY), :] = hx[0, pl.ds(c * CY, CY), :]
        v0[pl.ds(c * SPAN, CY), :] = hx[1, pl.ds(c * CY, CY), :]
    jac[pl.ds((CX + 1) * CY, CY), :] = hx[0, pl.ds(2 * CY, CY), :]
    jac[pl.ds(0, CY), :] = hx[1, pl.ds(2 * CY, CY), :]

    def star(buffer, base, halo, row, x):
        at = pl.multiple_of(base + (x + 1) * CY, CY)
        centre = buffer[pl.ds(at, CY), :]
        next_x = buffer[pl.ds(pl.multiple_of(at + CY, CY), CY), :]
        last_x = buffer[pl.ds(pl.multiple_of(at - CY, CY), CY), :]
        next_y = buffer[pl.ds(at + 1, CY), :]
        last_y = buffer[pl.ds(at - 1, CY), :]
        next_y = jnp.where(at_last, halo[0, pl.ds(row + x, 1), :], next_y)
        last_y = jnp.where(at_first, halo[1, pl.ds(row + x, 1), :], last_y)
        return centre, next_x, last_x, next_y, last_y

    def advance(buffer, halo, x):
        j, j_e, j_w, j_n, j_s = star(jac, 0, hy, 2 * CX, x)
        inverse = 1.0 / j
        k_e, k_w, k_n, k_s = j + j_e, j + j_w, j + j_n, j + j_s
        k_h = (time_step * viscosity * 0.5) * inverse
        k_v = (time_step * viscosity) * inverse * inverse
        stars = [star(buffer, c * SPAN, halo, c * CX, x) for c in range(2)]
        along = (-0.5 * time_step) * stars[0][0]
        across = (-0.5 * time_step) * stars[1][0]
        results = []
        for c in range(2):
            v, e, w, n, s = stars[c]
            spread = k_e * (e - v) + k_w * (w - v) + k_n * (n - v) + k_s * (s - v)
            above = jnp.where(top, 0.0, pltpu.roll(v, NZ - 1, 1))
            below = jnp.where(bottom, 0.0, pltpu.roll(v, 1, 1))
            change = along * (e - w) + across * (n - s) + k_h * spread + k_v * (above + below - 2.0 * v)
            results.append((v, change))
        return results

    def first_step(x, carry):
        for c, (v, change) in enumerate(advance(v0, hy, x)):
            new = v + change
            v1[pl.ds(pl.multiple_of(c * SPAN + (x + 1) * CY, CY), CY), :] = new
            cols[pl.ds(x * (4 * CY) + c, CY, stride=4), :] = v
            cols[pl.ds(x * (4 * CY) + 2 + c, CY, stride=4), :] = new
        return carry

    lax.fori_loop(0, CX, first_step, 0)

    cells_smem.wait()
    profile = prof_ref[...]

    def chunk(step, source):
        def some(g, carry):
            rows = []
            for u in range(16):
                where = cell_s[(step // SIDE) * 8 + u % 8, (step % SIDE) * BLOCK + g * 2 + u // 8]
                rows.append(cols[pl.ds(where, 4), :])
            for u in range(16):
                picked[pl.ds((g * 16 + u) * 4, 4), :] = rows[u]
            return carry

        lax.fori_loop(0, CAP // 16, some, 0)
        weights = source[pl.ds(pl.multiple_of(step * CAP, CAP), CAP), :]
        for q in range(5):
            if q < 4:
                product = picked[pl.ds(q, CAP, stride=4), :] * weights
            else:
                product = weights * profile
            product = product.reshape(BLOCK, 8, NZ)
            for level in range(5):
                product = fold(product, level)
            dots[pl.ds(q * GROUPS + step, 1)] = product

    chunk(0, wsend)

    def arrived(index, carry):
        step = nth(index)
        weight_copy(step).wait_recv()
        chunk(step, wrecv)
        return carry

    lax.fori_loop(0, GROUPS - 1, arrived, 0)
    sums = fold(fold(dots[...], 5), 6)
    sums = [sums[q * SIDE : (q + 1) * SIDE].reshape(2 * GROUPS, NZ) for q in range(5)]

    reynolds = meta_rey[...]

    def load_of(stress):
        pieces = [thirds(jnp.where(used, s, 0.0)) for s in stress]
        pieces = [[p.astype(f32) for p in piece] for piece in pieces]
        for j in range(2 * GROUPS):
            one = slice(j, j + 1)
            mask = iota((GROUPS, NZ), 0) == s_hi[one]
            parts = [jnp.where(mask, pieces[c][k][one], 0.0) for k in range(3) for c in range(2)]
            parts.append(jnp.zeros((2 * GROUPS, NZ), f32))
            a_slot[:, j * NZ : (j + 1) * NZ] = jnp.concatenate(parts, axis=0).astype(bf16)
        total = mm_nt(b_slot[...], a_slot[...])
        return total + pltpu.roll(total, NZ - 2 * GROUPS, 1) + pltpu.roll(total, NZ - 4 * GROUPS, 1)

    stress = wall_stress(sums[0], sums[1], reynolds)
    load = load_of(stress)
    for c in range(2):
        for block in range(CELLS // NZ):
            at = pl.ds(c * SPAN + CY + block * NZ, NZ)
            column = c * GROUPS + block
            v1[at, :] = v1[at, :] - load[:, column : column + 1] * profile

    edges(v1, None, ex2, ey2)
    halos2 = halo_copies(ex2, ey2, hx2, hy2, 4)
    for copy in halos2:
        copy.start()

    by_column = jnp.transpose(load)[0 : 2 * GROUPS]
    pieces = thirds(by_column)
    for j in range(2 * GROUPS):
        seen = b_slot[:, j * NZ : (j + 1) * NZ]
        spread = mm(pieces[0], seen) + mm(pieces[1], seen) + mm(pieces[2], seen)
        mask = iota((GROUPS, NZ), 0) == s_hi[j : j + 1]
        for c in range(2):
            at_face = jnp.where(mask, spread[c * GROUPS : (c + 1) * GROUPS], 0.0)
            loads[c, j : j + 1, :] = jnp.sum(at_face, axis=0, keepdims=True)
    stress = wall_stress(sums[2] - loads[0] * sums[4], sums[3] - loads[1] * sums[4], reynolds)
    for g in range(SIDE):
        eight = slice(g * 8, (g + 1) * 8)
        rsend[g] = jnp.concatenate([stress[0][eight], stress[1][eight]], axis=0)
    for step in range(1, GROUPS):
        stress_copy(step).start()

    load = load_of(stress)
    for c in range(2):
        for block in range(CELLS // NZ):
            at = pl.ds(c * SPAN + CY + block * NZ, NZ)
            column = c * GROUPS + block
            out[pl.ds(c * CELLS + block * NZ, NZ), :] = v1[at, :] - load[:, column : column + 1] * profile

    for copy in halos2:
        copy.wait_recv()
    for c in range(2):
        v1[pl.ds(c * SPAN + (CX + 1) * CY, CY), :] = hx2[0, pl.ds(c * CY, CY), :]
        v1[pl.ds(c * SPAN, CY), :] = hx2[1, pl.ds(c * CY, CY), :]

    def second_step(x, carry):
        for c, (v, change) in enumerate(advance(v1, hy2, x)):
            at = pl.ds(pl.multiple_of(c * CELLS + x * CY, CY), CY)
            out[at, :] = out[at, :] + change
        return carry

    lax.fori_loop(0, CX, second_step, 0)

    for step in range(1, GROUPS):
        stress_copy(step).wait_recv()
    back = jnp.concatenate([four(rsend[0], rrecv, g) for g in range(SIDE)], axis=0)
    pieces = thirds(back)
    for ch in range(chunks):
        one = slice(ch, ch + 1)
        span = slice(ch * NZ, (ch + 1) * NZ)
        seen = b_face[:, span]
        spread = mm(pieces[0], seen) + mm(pieces[1], seen) + mm(pieces[2], seen)
        place = hi_face[one, :]
        row = (place // 8) * 16 + place % 8
        for c in range(2):
            mask = iota((SIDE * 16, NZ), 0) == row + c * 8
            stress_out[c : c + 1, span] = jnp.sum(jnp.where(mask, spread, 0.0), axis=0, keepdims=True)

    for copy in halos + halos2:
        copy.wait_send()
    for step in range(1, GROUPS):
        meta_copy(step).wait_send()
        weight_copy(step).wait_send()
        stress_copy(step).wait_send()


def local(velocity, metric, weights, reynolds, face_tile, face_cell, profile):
    vm = pltpu.VMEM
    dma = pltpu.SemaphoreType.DMA
    small = (FACES // NZ, NZ)
    scratch = [
        vm((2 * SPAN, NZ), f32), vm((2 * SPAN, NZ), f32), vm((SPAN, NZ), f32), vm((FACES, NZ), f32),
        vm((SLOTS, NZ), f32), vm((SLOTS, NZ), f32),
        vm((SIDE, 16, NZ), f32), vm((GROUPS, 16, NZ), f32),
        vm(small, i32), vm(small, i32), vm((14 * GROUPS, FACES), bf16), vm((NZ, FACES), bf16),
        vm((2 * GROUPS, NZ), f32), vm((2 * GROUPS, NZ), f32),
        vm((2 * GROUPS, NZ), i32), pltpu.SMEM((2 * GROUPS, NZ), i32),
        vm((2 * GROUPS, NZ), i32), pltpu.SMEM((2 * GROUPS, NZ), i32),
        vm((4 * CELLS + 8, NZ), f32), vm((4 * CAP + 8, NZ), f32), vm((5 * GROUPS, 8, NZ), f32),
        vm((NZ, SLOTS), bf16), vm((NZ, SLOTS), bf16), vm((2, 2 * GROUPS, NZ), f32),
        vm((2, 3 * CY, NZ), f32), vm((2, 3 * CX, NZ), f32), vm((2, 2 * CY, NZ), f32), vm((2, 2 * CX, NZ), f32),
        vm((2, 3 * CY, NZ), f32), vm((2, 3 * CX, NZ), f32), vm((2, 2 * CY, NZ), f32), vm((2, 2 * CX, NZ), f32),
        vm((SIDE, 16, NZ), f32), vm((GROUPS, 16, NZ), f32),
        vm(small, f32), vm(small, i32), vm(small, i32), vm((1, NZ), f32),
        dma((8,)), dma((2,)), dma((GROUPS,)), dma((GROUPS,)), dma((GROUPS,)), dma((GROUPS,)),
        dma((8,)), dma((8,)), dma((GROUPS,)), dma((GROUPS,)),
    ]
    whole = pl.BlockSpec(memory_space=pltpu.HBM)
    inside = pl.BlockSpec(memory_space=pltpu.VMEM)
    out, stress = pl.pallas_call(
        kernel,
        out_shape=(
            jax.ShapeDtypeStruct((2 * CELLS, NZ), f32),
            jax.ShapeDtypeStruct((2, FACES), f32),
        ),
        in_specs=[whole] * 7,
        out_specs=(inside, inside),
        scratch_shapes=scratch,
        compiler_params=pltpu.CompilerParams(
            collective_id=0, has_side_effects=True, vmem_limit_bytes=48 * 1024 * 1024
        ),
    )(
        velocity.reshape(2 * CELLS, NZ), metric.reshape(CELLS, NZ), weights,
        reynolds.reshape(small), face_tile.reshape(small), face_cell.reshape(small), profile.reshape(1, NZ),
    )
    return out.reshape(2, CX, CY, NZ), stress


def solution(mesh):
    placed = (
        P(None, "gx", "gy", None),
        P("gx", "gy", None),
        P(("gx", "gy"), None),
        P(("gx", "gy")),
        P(("gx", "gy"), None),
        P(("gx", "gy")),
        P(),
    )
    return jax.shard_map(
        local,
        mesh=mesh,
        in_specs=placed,
        out_specs=(P(None, "gx", "gy", None), P(None, ("gx", "gy"))),
        check_vma=False,
    )
```

```python
import jax
import jax.numpy as jnp
from jax import lax
from jax.experimental import pallas as pl
from jax.experimental.pallas import tpu as pltpu
from jax.sharding import PartitionSpec as P

WALL_ITERS = 3
CAP = 256
CX = 64
CY = 32
NZ = 128
FACES = 2048
SIDE = 4
GROUPS = SIDE * SIDE
SLOTS = GROUPS * CAP
CELLS = CX * CY
SPAN = (CX + 2) * CY
BLOCK = CAP // 8

karman = 0.41
time_step = 0.2
viscosity = 0.5

MESH = pl.DeviceIdType.MESH
f32 = jnp.float32
bf16 = jnp.bfloat16
i32 = jnp.int32

NT = (((1,), (1,)), ((), ()))

ORDER = (0, 4, 12, 1, 3, 8, 2, 5, 15, 7, 13, 10, 6, 14, 9, 11)


def iota(shape, dim):
    return lax.broadcasted_iota(i32, shape, dim)


def mm(a, b):
    return jnp.dot(a, b, preferred_element_type=f32)


def mm_nt(a, b):
    return lax.dot_general(a, b, NT, preferred_element_type=f32)


def thirds(value):
    first = value.astype(bf16)
    rest = value - first.astype(f32)
    second = rest.astype(bf16)
    third = (rest - second.astype(f32)).astype(bf16)
    return first, second, third


def nth(index):
    words = [sum(step << (4 * k) for k, step in enumerate(ORDER[h : h + 4])) for h in (0, 4, 8, 12)]
    word = jnp.where(index < 8, jnp.where(index < 4, words[0], words[1]), jnp.where(index < 12, words[2], words[3]))
    return (word >> (4 * (index % 4))) & 15


def wall_stress(m0, m1, reynolds):
    speed = jnp.sqrt(m0 * m0 + m1 * m1 + 1.0)
    friction = 0.05 * speed
    for sweep in range(WALL_ITERS):
        friction = karman * speed / jnp.log(9.0 + reynolds * friction)
    factor = friction * friction / speed
    return factor * m0, factor * m1


def kernel(
    vel, met, wgt, rey_in, tile_in, cell_in, prof_in,
    out, stress_out,
    v0, v1, jac, win, wsend, wrecv, msend, mrecv, lo_face, hi_face, a_face, b_face,
    meta_cell, meta_rey, cell_v, cell_s, inv_v, inv_s, cols, picked, dots, b_slot, b_rows, a_slot, so_far, factors, loads,
    hx, hy, hx2, hy2, ex, ey, ex2, ey2, rsend, rrecv,
    rey_ref, tile_ref, cell_ref, prof_ref,
    in_sem, smem_sem, ms_sem, mr_sem, ws_sem, wr_sem, hs_sem, hr_sem, rs_sem, rr_sem,
):
    gx = lax.axis_index("gx")
    gy = lax.axis_index("gy")
    mz = gy // SIDE
    mx = gy % SIDE

    def peer(step):
        return ((mz + step // SIDE) % SIDE) * SIDE + (mx + step % SIDE) % SIDE

    def target(index):
        return peer(ORDER[index] if isinstance(index, int) else nth(index))

    def origin(index):
        step = ORDER[index]
        return peer(((SIDE - step // SIDE) % SIDE) * SIDE + (SIDE - step % SIDE) % SIDE)

    n_gx = lax.axis_size("gx")
    east = (lax.rem(gx + 1, n_gx), gy)
    west = (lax.rem(gx + n_gx - 1, n_gx), gy)
    north = (gx, lax.rem(gy + 1, GROUPS))
    south = (gx, lax.rem(gy + GROUPS - 1, GROUPS))

    barrier = pltpu.get_barrier_semaphore()
    for step in range(1, GROUPS):
        pl.semaphore_signal(barrier, inc=1, device_id=(gx, peer(step)), device_id_type=MESH)
    for side in (east, west):
        pl.semaphore_signal(barrier, inc=1, device_id=side, device_id_type=MESH)

    small_in = [
        pltpu.make_async_copy(tile_in, tile_ref, in_sem.at[4]),
        pltpu.make_async_copy(cell_in, cell_ref, in_sem.at[5]),
        pltpu.make_async_copy(rey_in, rey_ref, in_sem.at[6]),
        pltpu.make_async_copy(prof_in, prof_ref, in_sem.at[7]),
    ]
    for copy in small_in:
        copy.start()
    loads_in = [
        pltpu.make_async_copy(wgt, win, in_sem.at[0]),
        pltpu.make_async_copy(vel.at[pl.ds(0, CELLS)], v0.at[pl.ds(CY, CELLS)], in_sem.at[1]),
        pltpu.make_async_copy(vel.at[pl.ds(CELLS, CELLS)], v0.at[pl.ds(SPAN + CY, CELLS)], in_sem.at[2]),
        pltpu.make_async_copy(met, jac.at[pl.ds(CY, CELLS)], in_sem.at[3]),
    ]
    for copy in loads_in:
        copy.start()

    for copy in small_in:
        copy.wait()
    chunks = FACES // NZ
    tile = tile_ref[...]
    away = (((tile // SIDE) - mz + SIDE) % SIDE) * SIDE + ((tile % SIDE) - mx + SIDE) % SIDE
    member = jnp.concatenate([(away == step).astype(f32) for step in ORDER], axis=0)
    member16 = member.astype(bf16)
    upto = (iota((NZ, NZ), 0) <= iota((NZ, NZ), 1)).astype(f32).astype(bf16)
    rows_i = iota((GROUPS * chunks, GROUPS * chunks), 0)
    cols_i = iota((GROUPS * chunks, GROUPS * chunks), 1)
    ahead = ((rows_i // chunks == cols_i // chunks) & (cols_i < rows_i)).astype(f32).astype(bf16)
    ones = jnp.ones((2 * NZ, NZ), bf16)
    earlier = mm(mm(ahead, member16).astype(bf16), ones[:NZ])
    rank = mm(member16, upto) + earlier
    order = jnp.zeros((chunks, NZ), f32)
    chunk_of = jnp.zeros((chunks, NZ), f32)
    for t in range(GROUPS):
        sl = slice(t * chunks, (t + 1) * chunks)
        order = order + member[sl] * rank[sl]
        chunk_of = chunk_of + member[sl] * float(t)
    order = order.astype(i32) - 1
    chunk_of = chunk_of.astype(i32)
    hi = (chunk_of // SIDE) * 8 + order % 8
    lo = (chunk_of % SIDE) * BLOCK + order // 8
    hi_face[...] = hi
    lo_face[...] = lo
    cell = cell_ref[...]
    cell_hi = (cell // NZ + 1).astype(f32)
    cell_lo = (cell % NZ).astype(f32)
    r1, r2, r3 = thirds(rey_ref[...])
    r1, r2, r3 = r1.astype(f32), r2.astype(f32), r3.astype(f32)
    lane_row = iota((1, NZ), 1).astype(f32)
    for ch in range(chunks):
        one = slice(ch, ch + 1)
        span = slice(ch * NZ, (ch + 1) * NZ)
        b_face[:, span] = (iota((NZ, NZ), 0) == lo[one]).astype(f32).astype(bf16)
        mask = iota((2 * GROUPS, NZ), 0) == hi[one]
        values = [
            jnp.full((1, NZ), float(ch), f32), lane_row, cell_hi[one], cell_lo[one], r1[one], r2[one], r3[one],
        ]
        a_face[:, span] = jnp.concatenate([jnp.where(mask, v, 0.0) for v in values], axis=0).astype(bf16)
    table = mm_nt(a_face[...], b_face[...])
    part = [table[q * 2 * GROUPS : (q + 1) * 2 * GROUPS] for q in range(7)]
    inv_v[...] = jnp.clip((part[0] * float(NZ) + part[1]).astype(i32), 0, FACES - 1)
    slot_cell = jnp.where(part[2] > 0.0, (part[2] - 1.0) * float(NZ) + part[3], -1.0)
    slot_rey = (part[4] + part[5]) + part[6]
    to_smem = pltpu.make_async_copy(inv_v, inv_s, smem_sem.at[0])
    to_smem.start()
    for g in range(SIDE):
        eight = slice(g * 8, (g + 1) * 8)
        msend[g] = jnp.concatenate([slot_cell[eight], slot_rey[eight]], axis=0)

    def meta_copy(step):
        return pltpu.make_async_remote_copy(
            src_ref=msend.at[step // SIDE], dst_ref=mrecv.at[step],
            send_sem=ms_sem.at[step], recv_sem=mr_sem.at[step],
            device_id=(gx, target(step)), device_id_type=MESH,
        )

    def weight_copy(step):
        return pltpu.make_async_remote_copy(
            src_ref=wsend.at[pl.ds(step * CAP, CAP)], dst_ref=wrecv.at[pl.ds(step * CAP, CAP)],
            send_sem=ws_sem.at[step], recv_sem=wr_sem.at[step],
            device_id=(gx, target(step)), device_id_type=MESH,
        )

    def stress_copy(step):
        return pltpu.make_async_remote_copy(
            src_ref=rsend.at[step // SIDE], dst_ref=rrecv.at[step],
            send_sem=rs_sem.at[step], recv_sem=rr_sem.at[step],
            device_id=(gx, origin(step)),
            device_id_type=MESH,
        )

    def gather(table, step, source, rows, target, first):
        where = table.at[pl.ds((step // SIDE) * 8, 8), pl.ds((step % SIDE) * BLOCK, BLOCK)]
        for v in range(0, BLOCK, 4):
            places = [(k % 8, v + k // 8) for k in range(32)]
            runs = [source[pl.ds(where[place], rows), :] for place in places]
            for k, run in enumerate(runs):
                target[pl.ds(first + (v * 8 + k) * rows, rows), :] = run

    def pack(step):
        gather(inv_s, step, win, 1, wsend, step * CAP)

    def pack_send(step, carry):
        pack(step)
        weight_copy(step).start()
        return carry

    to_smem.wait()
    loads_in[0].wait()
    pack(1)

    pl.semaphore_wait(barrier, GROUPS + 1)
    for step in range(1, GROUPS):
        meta_copy(step).start()
    weight_copy(1).start()
    lax.fori_loop(2, 5, pack_send, 0)

    for copy in loads_in[1:]:
        copy.wait()

    def edges(buffer, jacobian, x_edge, y_edge):
        for n, at in enumerate((CY, CX * CY)):
            for c in range(2):
                x_edge[n, pl.ds(c * CY, CY), :] = buffer[pl.ds(c * SPAN + at, CY), :]
            if jacobian is not None:
                x_edge[n, pl.ds(2 * CY, CY), :] = jacobian[pl.ds(at, CY), :]
        for n, at in enumerate((CY, CY + CY - 1)):
            for c in range(2):
                y_edge[n, pl.ds(c * CX, CX), :] = buffer[pl.ds(c * SPAN + at, CX, stride=CY), :]
            if jacobian is not None:
                y_edge[n, pl.ds(2 * CX, CX), :] = jacobian[pl.ds(at, CX, stride=CY), :]

    def halo_copies(x_edge, y_edge, x_halo, y_halo, base):
        made = []
        for n, (edge, halo, way, device) in enumerate((
            (x_edge, x_halo, 0, west), (x_edge, x_halo, 1, east),
            (y_edge, y_halo, 0, south), (y_edge, y_halo, 1, north),
        )):
            made.append(pltpu.make_async_remote_copy(
                src_ref=edge.at[way], dst_ref=halo.at[way],
                send_sem=hs_sem.at[base + n], recv_sem=hr_sem.at[base + n],
                device_id=device, device_id_type=MESH,
            ))
        return made

    edges(v0, jac, ex, ey)
    halos = halo_copies(ex, ey, hx, hy, 0)
    for copy in halos:
        copy.start()

    lax.fori_loop(5, GROUPS, pack_send, 0)
    pack(0)

    for step in range(1, GROUPS):
        meta_copy(step).wait_recv()
    lanes16 = iota((16, NZ), 1) // BLOCK

    def four(first, received, g):
        rows = first if g == 0 else received[g * SIDE]
        for k in range(1, SIDE):
            rows = jnp.where(lanes16 == k, received[g * SIDE + k], rows)
        return rows

    for g in range(SIDE):
        rows = four(msend[0], mrecv, g)
        meta_cell[g * 8 : (g + 1) * 8, :] = rows[0:8]
        meta_rey[g * 8 : (g + 1) * 8, :] = rows[8:16]
    slot_of = meta_cell[...].astype(i32)
    cell_v[...] = jnp.clip(slot_of, 0, CELLS - 1) * 4
    cells_smem = pltpu.make_async_copy(cell_v, cell_s, smem_sem.at[1])
    cells_smem.start()
    used = slot_of >= 0
    s_hi = jnp.where(used, slot_of // NZ, -1)
    s_lo = jnp.where(used, slot_of % NZ, -1)
    for j in range(2 * GROUPS):
        seen = (iota((NZ, NZ), 0) == s_lo[j : j + 1]).astype(f32)
        b_slot[:, j * NZ : (j + 1) * NZ] = seen.astype(bf16)
        b_rows[j * NZ : (j + 1) * NZ, :] = jnp.transpose(seen).astype(bf16)

    for copy in halos:
        copy.wait_recv()

    row_y = iota((CY, NZ), 0)
    lane = iota((CY, NZ), 1)
    at_first, at_last = row_y == 0, row_y == CY - 1
    top, bottom = lane == NZ - 1, lane == 0

    for c in range(2):
        v0[pl.ds(c * SPAN + (CX + 1) * CY, CY), :] = hx[0, pl.ds(c * CY, CY), :]
        v0[pl.ds(c * SPAN, CY), :] = hx[1, pl.ds(c * CY, CY), :]
    jac[pl.ds((CX + 1) * CY, CY), :] = hx[0, pl.ds(2 * CY, CY), :]
    jac[pl.ds(0, CY), :] = hx[1, pl.ds(2 * CY, CY), :]

    def star(buffer, base, halo, row, x):
        at = pl.multiple_of(base + (x + 1) * CY, CY)
        centre = buffer[pl.ds(at, CY), :]
        next_x = buffer[pl.ds(pl.multiple_of(at + CY, CY), CY), :]
        last_x = buffer[pl.ds(pl.multiple_of(at - CY, CY), CY), :]
        next_y = buffer[pl.ds(at + 1, CY), :]
        last_y = buffer[pl.ds(at - 1, CY), :]
        next_y = jnp.where(at_last, halo[0, pl.ds(row + x, 1), :], next_y)
        last_y = jnp.where(at_first, halo[1, pl.ds(row + x, 1), :], last_y)
        return centre, next_x, last_x, next_y, last_y

    def column_sum(v):
        above = jnp.where(top, 0.0, pltpu.roll(v, NZ - 1, 1))
        below = jnp.where(bottom, 0.0, pltpu.roll(v, 1, 1))
        return above + below

    def first_step(x, carry):
        j, j_e, j_w, j_n, j_s = star(jac, 0, hy, 2 * CX, x)
        inverse = 1.0 / j
        k_h = (time_step * viscosity * 0.5) * inverse
        k_v = (time_step * viscosity) * inverse * inverse
        k_e, k_w, k_n, k_s = k_h * (j + j_e), k_h * (j + j_w), k_h * (j + j_n), k_h * (j + j_s)
        k_c = (k_e + k_w) + (k_n + k_s) + 2.0 * k_v
        at = pl.ds(pl.multiple_of(x * CY, CY), CY)
        for n, k in enumerate((k_e, k_w, k_n, k_s, k_v, k_c)):
            factors[n, at, :] = k
        stars = [star(v0, c * SPAN, hy, c * CX, x) for c in range(2)]
        along = (-0.5 * time_step) * stars[0][0]
        across = (-0.5 * time_step) * stars[1][0]
        k_e, k_w, k_n, k_s = k_e + along, k_w - along, k_n + across, k_s - across
        for c in range(2):
            v, e, w, n, s = stars[c]
            new = v + ((k_e * e + k_w * w) + (k_n * n + k_s * s) + (k_v * column_sum(v) - k_c * v))
            v1[pl.ds(pl.multiple_of(c * SPAN + (x + 1) * CY, CY), CY), :] = new
            cols[pl.ds(x * (4 * CY) + c, CY, stride=4), :] = v
            cols[pl.ds(x * (4 * CY) + 2 + c, CY, stride=4), :] = new
        return carry

    def second_step(x, carry):
        at = pl.ds(pl.multiple_of(x * CY, CY), CY)
        k_e, k_w, k_n, k_s, k_v, k_c = [factors[n, at, :] for n in range(6)]
        here = [pl.multiple_of(c * SPAN + (x + 1) * CY, CY) for c in range(2)]
        centre = [v1[pl.ds(here[c], CY), :] for c in range(2)]
        along = (-0.5 * time_step) * centre[0]
        across = (-0.5 * time_step) * centre[1]
        k_e, k_w = k_e + along, k_w - along
        k_n = jnp.where(at_last, 0.0, k_n + across)
        k_s = jnp.where(at_first, 0.0, k_s - across)
        for c in range(2):
            v = centre[c]
            e = v1[pl.ds(pl.multiple_of(here[c] + CY, CY), CY), :]
            w = v1[pl.ds(pl.multiple_of(here[c] - CY, CY), CY), :]
            n = v1[pl.ds(here[c] + 1, CY), :]
            s = v1[pl.ds(here[c] - 1, CY), :]
            change = (k_e * e + k_w * w) + (k_n * n + k_s * s) + (k_v * column_sum(v) - k_c * v)
            at = pl.ds(pl.multiple_of(c * CELLS + x * CY, CY), CY)
            out[at, :] = out[at, :] + change
        return carry

    lax.fori_loop(0, CX, first_step, 0)

    cells_smem.wait()
    profile = prof_ref[...]

    lane8 = iota((8, NZ), 1) % BLOCK

    def chunk(step, source):
        gather(cell_s, step, cols, 4, picked, 0)
        weights = source[pl.ds(pl.multiple_of(step * CAP, CAP), CAP), :]
        for q in range(5):
            if q < 4:
                product = picked[pl.ds(q, CAP, stride=4), :] * weights
            else:
                product = weights * profile
            total = jnp.sum(product, axis=1, keepdims=True)
            rows = jnp.zeros((8, NZ), f32)
            for v in range(BLOCK):
                rows = jnp.where(lane8 == v, total[v * 8 : (v + 1) * 8], rows)
            dots[pl.ds(q * GROUPS + step, 1)] = rows.reshape(1, 8, NZ)

    def arrived(step, carry):
        weight_copy(step).wait_recv()
        chunk(step, wrecv)
        return carry

    lanes8 = iota((8, NZ), 1) // BLOCK

    def group_sums(q, g):
        rows = dots[q * GROUPS + g * SIDE]
        for k in range(1, SIDE):
            rows = jnp.where(lanes8 == k, dots[q * GROUPS + g * SIDE + k], rows)
        return rows

    def group_load(stress, g):
        eight = slice(g * 8, (g + 1) * 8)
        pieces = [[p.astype(f32) for p in thirds(jnp.where(used[eight], s, 0.0))] for s in stress]
        for sub in range(8):
            one = slice(sub, sub + 1)
            mask = iota((GROUPS, NZ), 0) == s_hi[g * 8 + sub : g * 8 + sub + 1]
            parts = [jnp.where(mask, pieces[c][k][one], 0.0) for k in range(3) for c in range(2)]
            a_slot[:, sub * NZ : (sub + 1) * NZ] = jnp.concatenate(parts, axis=0).astype(bf16)
        total = mm(a_slot[...], b_rows[g * 8 * NZ : (g + 1) * 8 * NZ, :])
        width = 2 * GROUPS
        return (total[0:width] + total[width : 2 * width]) + total[2 * width : 3 * width]

    def by_cell(load):
        return jnp.transpose(jnp.concatenate([load, jnp.zeros((NZ - 2 * GROUPS, NZ), f32)], axis=0))

    reynolds = meta_rey[...]
    load = None
    for g in range(SIDE):
        if g == 0:
            chunk(0, wsend)
        lax.fori_loop(max(1, g * SIDE), (g + 1) * SIDE, arrived, 0)
        part = group_load(wall_stress(group_sums(0, g), group_sums(1, g), reynolds[g * 8 : (g + 1) * 8]), g)
        if g < SIDE - 1:
            so_far[...] = part if g == 0 else so_far[...] + part
        else:
            load = so_far[...] + part

    spread = by_cell(load)
    for c in range(2):
        for block in range(CELLS // NZ):
            at = pl.ds(c * SPAN + CY + block * NZ, NZ)
            column = c * GROUPS + block
            v1[at, :] = v1[at, :] - spread[:, column : column + 1] * profile

    edges(v1, None, ex2, ey2)
    halos2 = halo_copies(ex2, ey2, hx2, hy2, 4)
    for copy in halos2:
        copy.start()

    pieces = jnp.concatenate(thirds(load), axis=0)
    width = 2 * GROUPS
    for g in range(SIDE):
        seen = mm(pieces, b_slot[:, g * 8 * NZ : (g + 1) * 8 * NZ])
        seen = (seen[0:width] + seen[width : 2 * width]) + seen[2 * width : 3 * width]
        for sub in range(8):
            j = g * 8 + sub
            mask = iota((GROUPS, NZ), 0) == s_hi[j : j + 1]
            for c in range(2):
                at_face = jnp.where(mask, seen[c * GROUPS : (c + 1) * GROUPS, sub * NZ : (sub + 1) * NZ], 0.0)
                loads[c, j : j + 1, :] = jnp.sum(at_face, axis=0, keepdims=True)
    sums = [jnp.concatenate([group_sums(q, g) for g in range(SIDE)], axis=0) for q in range(2, 5)]
    stress = wall_stress(sums[0] - loads[0] * sums[2], sums[1] - loads[1] * sums[2], reynolds)
    for g in range(SIDE):
        eight = slice(g * 8, (g + 1) * 8)
        rsend[g] = jnp.concatenate([stress[0][eight], stress[1][eight]], axis=0)
    for step in range(1, GROUPS):
        stress_copy(step).start()

    load = None
    for g in range(SIDE):
        eight = slice(g * 8, (g + 1) * 8)
        part = group_load((stress[0][eight], stress[1][eight]), g)
        load = part if load is None else load + part
    spread = by_cell(load)
    for c in range(2):
        for block in range(CELLS // NZ):
            at = pl.ds(c * SPAN + CY + block * NZ, NZ)
            column = c * GROUPS + block
            out[pl.ds(c * CELLS + block * NZ, NZ), :] = v1[at, :] - spread[:, column : column + 1] * profile

    lax.fori_loop(1, CX - 1, second_step, 0)
    for copy in halos2:
        copy.wait_recv()
    for c in range(2):
        v1[pl.ds(c * SPAN + (CX + 1) * CY, CY), :] = hx2[0, pl.ds(c * CY, CY), :]
        v1[pl.ds(c * SPAN, CY), :] = hx2[1, pl.ds(c * CY, CY), :]
    second_step(0, 0)
    second_step(CX - 1, 0)
    for side, row, sign in ((0, CY - 1, 1.0), (1, 0, -1.0)):
        factor = factors[2 + side, pl.ds(row, CX, stride=CY), :]
        factor = factor + (sign * -0.5 * time_step) * v1[pl.ds(SPAN + CY + row, CX, stride=CY), :]
        for c in range(2):
            added = hy2[side, pl.ds(c * CX, CX), :] * factor
            most = CX - 8
            at = pl.ds(c * CELLS + row, most, stride=CY)
            out[at, :] = out[at, :] + added[:most]
            for x in range(most, CX):
                at = pl.ds(c * CELLS + row + x * CY, 1)
                out[at, :] = out[at, :] + added[x : x + 1]

    for step in range(1, GROUPS):
        stress_copy(step).wait_recv()
    back = jnp.concatenate([four(rsend[0], rrecv, g) for g in range(SIDE)], axis=0)
    pieces = jnp.concatenate(thirds(back), axis=0)
    width = SIDE * 16
    for ch in range(chunks):
        one = slice(ch, ch + 1)
        span = slice(ch * NZ, (ch + 1) * NZ)
        seen = b_face[:, span]
        spread = mm(pieces, seen)
        spread = (spread[0:width] + spread[width : 2 * width]) + spread[2 * width : 3 * width]
        place = hi_face[one, :]
        row = (place // 8) * 16 + place % 8
        for c in range(2):
            mask = iota((SIDE * 16, NZ), 0) == row + c * 8
            stress_out[c : c + 1, span] = jnp.sum(jnp.where(mask, spread, 0.0), axis=0, keepdims=True)

    for copy in halos + halos2:
        copy.wait_send()
    for step in range(1, GROUPS):
        meta_copy(step).wait_send()
        weight_copy(step).wait_send()
        stress_copy(step).wait_send()


def local(velocity, metric, weights, reynolds, face_tile, face_cell, profile):
    vm = pltpu.VMEM
    dma = pltpu.SemaphoreType.DMA
    small = (FACES // NZ, NZ)
    scratch = [
        vm((2 * SPAN, NZ), f32), vm((2 * SPAN, NZ), f32), vm((SPAN, NZ), f32), vm((FACES, NZ), f32),
        vm((SLOTS, NZ), f32), vm((SLOTS, NZ), f32),
        vm((SIDE, 16, NZ), f32), vm((GROUPS, 16, NZ), f32),
        vm(small, i32), vm(small, i32), vm((14 * GROUPS, FACES), bf16), vm((NZ, FACES), bf16),
        vm((2 * GROUPS, NZ), f32), vm((2 * GROUPS, NZ), f32),
        vm((2 * GROUPS, NZ), i32), pltpu.SMEM((2 * GROUPS, NZ), i32),
        vm((2 * GROUPS, NZ), i32), pltpu.SMEM((2 * GROUPS, NZ), i32),
        vm((4 * CELLS + 8, NZ), f32), vm((4 * CAP + 8, NZ), f32), vm((5 * GROUPS, 8, NZ), f32),
        vm((NZ, SLOTS), bf16), vm((SLOTS, NZ), bf16), vm((6 * GROUPS, 8 * NZ), bf16), vm((2 * GROUPS, NZ), f32),
        vm((6, CELLS + CY, NZ), f32), vm((2, 2 * GROUPS, NZ), f32),
        vm((2, 3 * CY, NZ), f32), vm((2, 3 * CX, NZ), f32), vm((2, 2 * CY, NZ), f32), vm((2, 2 * CX, NZ), f32),
        vm((2, 3 * CY, NZ), f32), vm((2, 3 * CX, NZ), f32), vm((2, 2 * CY, NZ), f32), vm((2, 2 * CX, NZ), f32),
        vm((SIDE, 16, NZ), f32), vm((GROUPS, 16, NZ), f32),
        vm(small, f32), vm(small, i32), vm(small, i32), vm((1, NZ), f32),
        dma((8,)), dma((2,)), dma((GROUPS,)), dma((GROUPS,)), dma((GROUPS,)), dma((GROUPS,)),
        dma((8,)), dma((8,)), dma((GROUPS,)), dma((GROUPS,)),
    ]
    whole = pl.BlockSpec(memory_space=pltpu.HBM)
    inside = pl.BlockSpec(memory_space=pltpu.VMEM)
    out, stress = pl.pallas_call(
        kernel,
        out_shape=(
            jax.ShapeDtypeStruct((2 * CELLS, NZ), f32),
            jax.ShapeDtypeStruct((2, FACES), f32),
        ),
        in_specs=[whole] * 7,
        out_specs=(inside, inside),
        scratch_shapes=scratch,
        compiler_params=pltpu.CompilerParams(
            collective_id=0, has_side_effects=True, vmem_limit_bytes=58 * 1024 * 1024
        ),
    )(
        velocity.reshape(2 * CELLS, NZ), metric.reshape(CELLS, NZ), weights,
        reynolds.reshape(small), face_tile.reshape(small), face_cell.reshape(small), profile.reshape(1, NZ),
    )
    return out.reshape(2, CX, CY, NZ), stress


def solution(mesh):
    placed = (
        P(None, "gx", "gy", None),
        P("gx", "gy", None),
        P(("gx", "gy"), None),
        P(("gx", "gy")),
        P(("gx", "gy"), None),
        P(("gx", "gy")),
        P(),
    )
    return jax.shard_map(
        local,
        mesh=mesh,
        in_specs=placed,
        out_specs=(P(None, "gx", "gy", None), P(None, ("gx", "gy"))),
        check_vma=False,
    )
```

```python
import jax
import jax.numpy as jnp
from jax import lax
from jax.experimental import pallas as pl
from jax.experimental.pallas import tpu as pltpu
from jax.sharding import PartitionSpec as P

WALL_ITERS = 3
CAP = 256
CX = 64
CY = 32
NZ = 128
FACES = 2048
SIDE = 4
GROUPS = SIDE * SIDE
SLOTS = GROUPS * CAP
CELLS = CX * CY
SPAN = (CX + 2) * CY
BLOCK = CAP // 8
RUN = 4

karman = 0.41
time_step = 0.2
viscosity = 0.5

MESH = pl.DeviceIdType.MESH
f32 = jnp.float32
bf16 = jnp.bfloat16
i32 = jnp.int32

NT = (((1,), (1,)), ((), ()))

ORDER = (0, 4, 12, 1, 3, 8, 2, 5, 15, 7, 13, 10, 6, 14, 9, 11)


def iota(shape, dim):
    return lax.broadcasted_iota(i32, shape, dim)


def mm(a, b):
    return jnp.dot(a, b, preferred_element_type=f32)


def mm_nt(a, b):
    return lax.dot_general(a, b, NT, preferred_element_type=f32)


def thirds(value):
    first = value.astype(bf16)
    rest = value - first.astype(f32)
    second = rest.astype(bf16)
    third = (rest - second.astype(f32)).astype(bf16)
    return first, second, third


def nth(index):
    words = [sum(step << (4 * k) for k, step in enumerate(ORDER[h : h + 4])) for h in (0, 4, 8, 12)]
    word = jnp.where(index < 8, jnp.where(index < 4, words[0], words[1]), jnp.where(index < 12, words[2], words[3]))
    return (word >> (4 * (index % 4))) & 15


def wall_stress(m0, m1, reynolds):
    speed = jnp.sqrt(m0 * m0 + m1 * m1 + 1.0)
    friction = 0.05 * speed
    for sweep in range(WALL_ITERS):
        friction = karman * speed / jnp.log(9.0 + reynolds * friction)
    factor = friction * friction / speed
    return factor * m0, factor * m1


def kernel(
    vel, met, wgt, rey_in, tile_in, cell_in, prof_in,
    out, stress_out,
    v0, v1, jac, win, wsend, wrecv, msend, mrecv, lo_face, hi_face, a_face, b_face,
    meta_cell, meta_rey, cell_v, cell_s, inv_v, inv_s, cols, picked, dots, b_slot, b_rows, a_slot, so_far, factors, slot_hi,
    hx, hy, hx2, hy2, ex, ey, ex2, ey2, rsend, rrecv,
    rey_ref, tile_ref, cell_ref, prof_ref,
    in_sem, smem_sem, ms_sem, mr_sem, ws_sem, wr_sem, hs_sem, hr_sem, rs_sem, rr_sem,
):
    gx = lax.axis_index("gx")
    gy = lax.axis_index("gy")
    mz = gy // SIDE
    mx = gy % SIDE

    def peer(step):
        return ((mz + step // SIDE) % SIDE) * SIDE + (mx + step % SIDE) % SIDE

    def target(index):
        return peer(ORDER[index] if isinstance(index, int) else nth(index))

    def origin(index):
        step = ORDER[index]
        return peer(((SIDE - step // SIDE) % SIDE) * SIDE + (SIDE - step % SIDE) % SIDE)

    n_gx = lax.axis_size("gx")
    east = (lax.rem(gx + 1, n_gx), gy)
    west = (lax.rem(gx + n_gx - 1, n_gx), gy)
    north = (gx, lax.rem(gy + 1, GROUPS))
    south = (gx, lax.rem(gy + GROUPS - 1, GROUPS))

    barrier = pltpu.get_barrier_semaphore()
    for step in range(1, GROUPS):
        pl.semaphore_signal(barrier, inc=1, device_id=(gx, peer(step)), device_id_type=MESH)
    for side in (east, west):
        pl.semaphore_signal(barrier, inc=1, device_id=side, device_id_type=MESH)

    small_in = [
        pltpu.make_async_copy(tile_in, tile_ref, in_sem.at[4]),
        pltpu.make_async_copy(cell_in, cell_ref, in_sem.at[5]),
        pltpu.make_async_copy(rey_in, rey_ref, in_sem.at[6]),
        pltpu.make_async_copy(prof_in, prof_ref, in_sem.at[7]),
    ]
    for copy in small_in:
        copy.start()
    loads_in = [
        pltpu.make_async_copy(wgt, win, in_sem.at[0]),
        pltpu.make_async_copy(vel.at[pl.ds(0, CELLS)], v0.at[pl.ds(CY, CELLS)], in_sem.at[1]),
        pltpu.make_async_copy(vel.at[pl.ds(CELLS, CELLS)], v0.at[pl.ds(SPAN + CY, CELLS)], in_sem.at[2]),
        pltpu.make_async_copy(met, jac.at[pl.ds(CY, CELLS)], in_sem.at[3]),
    ]
    for copy in loads_in:
        copy.start()

    for copy in small_in:
        copy.wait()
    chunks = FACES // NZ
    tile = tile_ref[...]
    away = (((tile // SIDE) - mz + SIDE) % SIDE) * SIDE + ((tile % SIDE) - mx + SIDE) % SIDE
    member = jnp.concatenate([(away == step).astype(f32) for step in ORDER], axis=0)
    member16 = member.astype(bf16)
    upto = (iota((NZ, NZ), 0) <= iota((NZ, NZ), 1)).astype(f32).astype(bf16)
    rows_i = iota((GROUPS * chunks, GROUPS * chunks), 0)
    cols_i = iota((GROUPS * chunks, GROUPS * chunks), 1)
    ahead = ((rows_i // chunks == cols_i // chunks) & (cols_i < rows_i)).astype(f32).astype(bf16)
    ones = jnp.ones((2 * NZ, NZ), bf16)
    earlier = mm(mm(ahead, member16).astype(bf16), ones[:NZ])
    rank = mm(member16, upto) + earlier
    order = jnp.zeros((chunks, NZ), f32)
    chunk_of = jnp.zeros((chunks, NZ), f32)
    for t in range(GROUPS):
        sl = slice(t * chunks, (t + 1) * chunks)
        order = order + member[sl] * rank[sl]
        chunk_of = chunk_of + member[sl] * float(t)
    order = order.astype(i32) - 1
    chunk_of = chunk_of.astype(i32)
    hi = (chunk_of // SIDE) * 8 + order % 8
    lo = (chunk_of % SIDE) * BLOCK + order // 8
    hi_face[...] = hi
    lo_face[...] = lo
    cell = cell_ref[...]
    cell_hi = (cell // NZ + 1).astype(f32)
    cell_lo = (cell % NZ).astype(f32)
    r1, r2, r3 = thirds(rey_ref[...])
    r1, r2, r3 = r1.astype(f32), r2.astype(f32), r3.astype(f32)
    lane_row = iota((1, NZ), 1).astype(f32)
    for ch in range(chunks):
        one = slice(ch, ch + 1)
        span = slice(ch * NZ, (ch + 1) * NZ)
        b_face[:, span] = (iota((NZ, NZ), 0) == lo[one]).astype(f32).astype(bf16)
        mask = iota((2 * GROUPS, NZ), 0) == hi[one]
        values = [
            jnp.full((1, NZ), float(ch), f32), lane_row, cell_hi[one], cell_lo[one], r1[one], r2[one], r3[one],
        ]
        a_face[:, span] = jnp.concatenate([jnp.where(mask, v, 0.0) for v in values], axis=0).astype(bf16)
    table = mm_nt(a_face[...], b_face[...])
    part = [table[q * 2 * GROUPS : (q + 1) * 2 * GROUPS] for q in range(7)]
    inv_v[...] = jnp.clip((part[0] * float(NZ) + part[1]).astype(i32), 0, FACES - 1)
    slot_cell = jnp.where(part[2] > 0.0, (part[2] - 1.0) * float(NZ) + part[3], -1.0)
    slot_rey = (part[4] + part[5]) + part[6]
    to_smem = pltpu.make_async_copy(inv_v, inv_s, smem_sem.at[0])
    to_smem.start()
    lanes8 = iota((8, NZ), 1) // BLOCK
    for g in range(SIDE):
        eight = slice(g * 8, (g + 1) * 8)
        beside = pltpu.roll(slot_rey[eight], BLOCK, 1)
        for k in range(SIDE):
            msend[g * SIDE + k] = jnp.where(lanes8 == k, slot_cell[eight], beside)

    def meta_copy(step):
        return pltpu.make_async_remote_copy(
            src_ref=msend.at[step], dst_ref=mrecv.at[step],
            send_sem=ms_sem.at[step], recv_sem=mr_sem.at[step],
            device_id=(gx, target(step)), device_id_type=MESH,
        )

    def weight_copy(step):
        return pltpu.make_async_remote_copy(
            src_ref=wsend.at[pl.ds(step * CAP, CAP)], dst_ref=wrecv.at[pl.ds(step * CAP, CAP)],
            send_sem=ws_sem.at[step], recv_sem=wr_sem.at[step],
            device_id=(gx, target(step)), device_id_type=MESH,
        )

    def stress_copy(step):
        return pltpu.make_async_remote_copy(
            src_ref=rsend.at[step], dst_ref=rrecv.at[step],
            send_sem=rs_sem.at[step], recv_sem=rr_sem.at[step],
            device_id=(gx, origin(step)),
            device_id_type=MESH,
        )

    def gather(table, step, source, rows, target, first):
        where = table.at[pl.ds((step // SIDE) * 8, 8), pl.ds((step % SIDE) * BLOCK, BLOCK)]
        for v in range(0, BLOCK, 4):
            places = [(k % 8, v + k // 8) for k in range(32)]
            runs = [source[pl.ds(where[place], rows), :] for place in places]
            for k, run in enumerate(runs):
                target[pl.ds(first + (v * 8 + k) * rows, rows), :] = run

    to_smem.wait()
    loads_in[0].wait()
    gather(inv_s, 1, win, 1, wsend, CAP)

    pl.semaphore_wait(barrier, GROUPS + 1)
    for step in range(1, GROUPS):
        meta_copy(step).start()
    weight_copy(1).start()


    def edges(buffer, jacobian, x_edge, y_edge):
        for n, at in enumerate((CY, CX * CY)):
            for c in range(2):
                x_edge[n, pl.ds(c * CY, CY), :] = buffer[pl.ds(c * SPAN + at, CY), :]
            if jacobian is not None:
                x_edge[n, pl.ds(2 * CY, CY), :] = jacobian[pl.ds(at, CY), :]
        for n, at in enumerate((CY, CY + CY - 1)):
            for c in range(2):
                y_edge[n, pl.ds(c * CX, CX), :] = buffer[pl.ds(c * SPAN + at, CX, stride=CY), :]
            if jacobian is not None:
                y_edge[n, pl.ds(2 * CX, CX), :] = jacobian[pl.ds(at, CX, stride=CY), :]

    def halo_copies(x_edge, y_edge, x_halo, y_halo, base):
        made = []
        for n, (edge, halo, way, device) in enumerate((
            (x_edge, x_halo, 0, west), (x_edge, x_halo, 1, east),
            (y_edge, y_halo, 0, south), (y_edge, y_halo, 1, north),
        )):
            made.append(pltpu.make_async_remote_copy(
                src_ref=edge.at[way], dst_ref=halo.at[way],
                send_sem=hs_sem.at[base + n], recv_sem=hr_sem.at[base + n],
                device_id=device, device_id_type=MESH,
            ))
        return made

    halos = halo_copies(ex, ey, hx, hy, 0)

    def pack_send(step, carry):
        gather(inv_s, step, win, 1, wsend, step * CAP)
        weight_copy(step).start()

        @pl.when(step == 4)
        def _():
            for copy in loads_in[1:]:
                copy.wait()
            edges(v0, jac, ex, ey)
            for copy in halos:
                copy.start()

        return carry

    lax.fori_loop(2, GROUPS, pack_send, 0)
    gather(inv_s, 0, win, 1, wrecv, 0)

    for step in range(1, GROUPS):
        meta_copy(step).wait_recv()

    def four(first, received, g):
        tiles = [first if g + k == 0 else received[g * SIDE + k] for k in range(SIDE)]
        rows, others = tiles[0], tiles[SIDE - 1]
        for k in range(1, SIDE):
            rows = jnp.where(lanes8 == k, tiles[k], rows)
            others = jnp.where(lanes8 == k, tiles[k - 1], others)
        return rows, pltpu.roll(others, NZ - BLOCK, 1)

    for g in range(SIDE):
        rows, others = four(msend[0], mrecv, g)
        meta_cell[g * 8 : (g + 1) * 8, :] = rows
        meta_rey[g * 8 : (g + 1) * 8, :] = others
    slot_of = meta_cell[...].astype(i32)
    cell_v[...] = jnp.clip(slot_of, 0, CELLS - 1) * 4
    cells_smem = pltpu.make_async_copy(cell_v, cell_s, smem_sem.at[1])
    cells_smem.start()
    used = slot_of >= 0
    s_hi = jnp.where(used, slot_of // NZ, -1)
    slot_hi[...] = s_hi
    s_lo = jnp.where(used, slot_of % NZ, -1)
    for j in range(2 * GROUPS):
        seen = (iota((NZ, NZ), 0) == s_lo[j : j + 1]).astype(f32)
        b_slot[:, j * NZ : (j + 1) * NZ] = seen.astype(bf16)
        b_rows[j * NZ : (j + 1) * NZ, :] = jnp.transpose(seen).astype(bf16)

    for copy in halos:
        copy.wait_recv()

    row_y = iota((CY, NZ), 0)
    lane = iota((CY, NZ), 1)
    at_first, at_last = row_y == 0, row_y == CY - 1

    for c in range(2):
        v0[pl.ds(c * SPAN + (CX + 1) * CY, CY), :] = hx[0, pl.ds(c * CY, CY), :]
        v0[pl.ds(c * SPAN, CY), :] = hx[1, pl.ds(c * CY, CY), :]
    jac[pl.ds((CX + 1) * CY, CY), :] = hx[0, pl.ds(2 * CY, CY), :]
    jac[pl.ds(0, CY), :] = hx[1, pl.ds(2 * CY, CY), :]

    def star(buffer, base, halo, row, x):
        at = pl.multiple_of(base + (x + 1) * CY, CY)
        centre = buffer[pl.ds(at, CY), :]
        next_x = buffer[pl.ds(pl.multiple_of(at + CY, CY), CY), :]
        last_x = buffer[pl.ds(pl.multiple_of(at - CY, CY), CY), :]
        next_y = buffer[pl.ds(at + 1, CY), :]
        last_y = buffer[pl.ds(at - 1, CY), :]
        next_y = jnp.where(at_last, halo[0, pl.ds(row + x, 1), :], next_y)
        last_y = jnp.where(at_first, halo[1, pl.ds(row + x, 1), :], last_y)
        return centre, next_x, last_x, next_y, last_y

    def column_sum(v, level):
        above = jnp.where(level == NZ - 1, 0.0, pltpu.roll(v, NZ - 1, 1))
        below = jnp.where(level == 0, 0.0, pltpu.roll(v, 1, 1))
        return above + below

    def first_step(x, carry):
        j, j_e, j_w, j_n, j_s = star(jac, 0, hy, 2 * CX, x)
        inverse = 1.0 / j
        k_h = (time_step * viscosity * 0.5) * inverse
        k_v = (time_step * viscosity) * inverse * inverse
        k_e, k_w, k_n, k_s = k_h * (j + j_e), k_h * (j + j_w), k_h * (j + j_n), k_h * (j + j_s)
        k_c = (k_e + k_w) + (k_n + k_s) + 2.0 * k_v
        at = pl.ds(pl.multiple_of(x * CY, CY), CY)
        for n, k in enumerate((k_e, k_w, k_n, k_s, k_v, k_c)):
            factors[n, at, :] = k
        stars = [star(v0, c * SPAN, hy, c * CX, x) for c in range(2)]
        along = (-0.5 * time_step) * stars[0][0]
        across = (-0.5 * time_step) * stars[1][0]
        k_e, k_w, k_n, k_s = k_e + along, k_w - along, k_n + across, k_s - across
        for c in range(2):
            v, e, w, n, s = stars[c]
            new = v + ((k_e * e + k_w * w) + (k_n * n + k_s * s) + (k_v * column_sum(v, lane) - k_c * v))
            v1[pl.ds(pl.multiple_of(c * SPAN + (x + 1) * CY, CY), CY), :] = new
            cols[pl.ds(x * (4 * CY) + c, CY, stride=4), :] = v
            cols[pl.ds(x * (4 * CY) + 2 + c, CY, stride=4), :] = new
        return carry

    tall = RUN * CY
    y_tall, lane_tall = iota((tall, NZ), 0) % CY, iota((tall, NZ), 1)

    def second_step(run, carry):
        x = run * RUN
        at = pl.ds(pl.multiple_of(x * CY, tall), tall)
        k_e, k_w, k_n, k_s, k_v, k_c = [factors[n, at, :] for n in range(6)]
        here = [pl.multiple_of(c * SPAN + (x + 1) * CY, CY) for c in range(2)]
        centre = [v1[pl.ds(here[c], tall), :] for c in range(2)]
        along = (-0.5 * time_step) * centre[0]
        across = (-0.5 * time_step) * centre[1]
        k_e, k_w = k_e + along, k_w - along
        k_n = jnp.where(y_tall == CY - 1, 0.0, k_n + across)
        k_s = jnp.where(y_tall == 0, 0.0, k_s - across)
        for c in range(2):
            v = centre[c]
            e = v1[pl.ds(pl.multiple_of(here[c] + CY, CY), tall), :]
            w = v1[pl.ds(pl.multiple_of(here[c] - CY, CY), tall), :]
            n = v1[pl.ds(here[c] + 1, tall), :]
            s = v1[pl.ds(here[c] - 1, tall), :]
            change = (k_e * e + k_w * w) + (k_n * n + k_s * s) + (k_v * column_sum(v, lane_tall) - k_c * v)
            at = pl.ds(pl.multiple_of(c * CELLS + x * CY, tall), tall)
            out[at, :] = out[at, :] + change
        return carry

    def first_pair(pair, carry):
        return first_step(2 * pair + 1, first_step(2 * pair, carry))

    lax.fori_loop(0, CX // 2, first_pair, 0)

    cells_smem.wait()
    profile = prof_ref[...]

    lane8 = iota((8, NZ), 1) % BLOCK

    def chunk(step):
        gather(cell_s, step, cols, 4, picked, 0)
        weights = wrecv[pl.ds(pl.multiple_of(step * CAP, CAP), CAP), :]
        for q in range(5):
            if q < 4:
                product = picked[pl.ds(q, CAP, stride=4), :] * weights
            else:
                product = weights * profile
            total = jnp.sum(product, axis=1, keepdims=True)
            rows = jnp.zeros((8, NZ), f32)
            for v in range(BLOCK):
                rows = jnp.where(lane8 == v, total[v * 8 : (v + 1) * 8], rows)
            dots[pl.ds(q * GROUPS + step, 1)] = rows.reshape(1, 8, NZ)

    def arrived(step, carry):
        @pl.when(step > 0)
        def _():
            weight_copy(step).wait_recv()

        chunk(step)
        return carry

    def group_sums(q, g):
        rows = dots[q * GROUPS + g * SIDE]
        for k in range(1, SIDE):
            rows = jnp.where(lanes8 == k, dots[q * GROUPS + g * SIDE + k], rows)
        return rows

    def eight_rows(ref, g):
        return ref[pl.ds(g * 8 if isinstance(g, int) else pl.multiple_of(g * 8, 8), 8), :]

    def group_load(stress, g):
        high = eight_rows(slot_hi, g)
        pieces = [[p.astype(f32) for p in thirds(jnp.where(high >= 0, s, 0.0))] for s in stress]
        for sub in range(8):
            one = slice(sub, sub + 1)
            mask = iota((GROUPS, NZ), 0) == high[one]
            parts = [jnp.where(mask, pieces[c][k][one], 0.0) for k in range(3) for c in range(2)]
            a_slot[:, sub * NZ : (sub + 1) * NZ] = jnp.concatenate(parts, axis=0).astype(bf16)
        total = mm(a_slot[...], b_rows[pl.ds((g * 8 * NZ if isinstance(g, int) else pl.multiple_of(g * 8 * NZ, 8 * NZ)), 8 * NZ), :])
        width = 2 * GROUPS
        so_far[...] = so_far[...] + ((total[0:width] + total[width : 2 * width]) + total[2 * width : 3 * width])

    def by_cell(load):
        return jnp.transpose(jnp.concatenate([load, jnp.zeros((NZ - 2 * GROUPS, NZ), f32)], axis=0))

    def group(g, carry):
        lax.fori_loop(g * SIDE, (g + 1) * SIDE, arrived, 0)
        group_load(wall_stress(group_sums(0, g), group_sums(1, g), eight_rows(meta_rey, g)), g)
        return carry

    so_far[...] = jnp.zeros((2 * GROUPS, NZ), f32)
    lax.fori_loop(0, SIDE, group, 0)
    load = so_far[...]

    spread = by_cell(load)
    for c in range(2):
        for block in range(CELLS // NZ):
            at = pl.ds(c * SPAN + CY + block * NZ, NZ)
            column = c * GROUPS + block
            v1[at, :] = v1[at, :] - spread[:, column : column + 1] * profile

    edges(v1, None, ex2, ey2)
    halos2 = halo_copies(ex2, ey2, hx2, hy2, 4)
    for copy in halos2:
        copy.start()

    pieces = jnp.concatenate(thirds(load), axis=0)
    width = 2 * GROUPS
    so_far[...] = jnp.zeros((2 * GROUPS, NZ), f32)

    def second_group(g, carry):
        high = eight_rows(slot_hi, g)
        seen = mm(pieces, b_slot[:, pl.ds((g * 8 * NZ if isinstance(g, int) else pl.multiple_of(g * 8 * NZ, 8 * NZ)), 8 * NZ)])
        seen = (seen[0:width] + seen[width : 2 * width]) + seen[2 * width : 3 * width]
        met_load = [[], []]
        for sub in range(8):
            mask = iota((GROUPS, NZ), 0) == high[sub : sub + 1]
            for c in range(2):
                at_face = jnp.where(mask, seen[c * GROUPS : (c + 1) * GROUPS, sub * NZ : (sub + 1) * NZ], 0.0)
                met_load[c].append(jnp.sum(at_face, axis=0, keepdims=True))
        met_load = [jnp.concatenate(rows, axis=0) for rows in met_load]
        shape = group_sums(4, g)
        stress = wall_stress(
            group_sums(2, g) - met_load[0] * shape, group_sums(3, g) - met_load[1] * shape, eight_rows(meta_rey, g)
        )
        beside = pltpu.roll(stress[1], BLOCK, 1)
        for k in range(SIDE):
            rsend[g * SIDE + k] = jnp.where(lanes8 == k, stress[0], beside)
        return stress

    stresses = [second_group(g, 0) for g in range(SIDE)]
    for step in range(1, GROUPS):
        stress_copy(step).start()
    for g in range(SIDE):
        group_load(stresses[g], g)

    load = so_far[...]
    spread = by_cell(load)
    for c in range(2):
        for block in range(CELLS // NZ):
            at = pl.ds(c * SPAN + CY + block * NZ, NZ)
            column = c * GROUPS + block
            out[pl.ds(c * CELLS + block * NZ, NZ), :] = v1[at, :] - spread[:, column : column + 1] * profile

    lax.fori_loop(1, CX // RUN - 1, second_step, 0)
    for copy in halos2:
        copy.wait_recv()
    for c in range(2):
        v1[pl.ds(c * SPAN + (CX + 1) * CY, CY), :] = hx2[0, pl.ds(c * CY, CY), :]
        v1[pl.ds(c * SPAN, CY), :] = hx2[1, pl.ds(c * CY, CY), :]
    lax.fori_loop(0, 2, lambda n, carry: second_step(n * (CX // RUN - 1), carry), 0)
    for side, row, sign in ((0, CY - 1, 1.0), (1, 0, -1.0)):
        factor = factors[2 + side, pl.ds(row, CX, stride=CY), :]
        factor = factor + (sign * -0.5 * time_step) * v1[pl.ds(SPAN + CY + row, CX, stride=CY), :]
        for c in range(2):
            added = hy2[side, pl.ds(c * CX, CX), :] * factor
            most = CX - 8
            at = pl.ds(c * CELLS + row, most, stride=CY)
            out[at, :] = out[at, :] + added[:most]
            for x in range(most, CX):
                at = pl.ds(c * CELLS + row + x * CY, 1)
                out[at, :] = out[at, :] + added[x : x + 1]

    for step in range(1, GROUPS):
        stress_copy(step).wait_recv()
    back = jnp.concatenate([rows for g in range(SIDE) for rows in four(rsend[0], rrecv, g)], axis=0)
    pieces = jnp.concatenate(thirds(back), axis=0)
    width = SIDE * 16
    for ch in range(chunks):
        one = slice(ch, ch + 1)
        span = slice(ch * NZ, (ch + 1) * NZ)
        seen = b_face[:, span]
        spread = mm(pieces, seen)
        spread = (spread[0:width] + spread[width : 2 * width]) + spread[2 * width : 3 * width]
        place = hi_face[one, :]
        row = (place // 8) * 16 + place % 8
        for c in range(2):
            mask = iota((SIDE * 16, NZ), 0) == row + c * 8
            stress_out[c : c + 1, span] = jnp.sum(jnp.where(mask, spread, 0.0), axis=0, keepdims=True)

    for copy in halos + halos2:
        copy.wait_send()
    for step in range(1, GROUPS):
        meta_copy(step).wait_send()
        weight_copy(step).wait_send()
        stress_copy(step).wait_send()


def local(velocity, metric, weights, reynolds, face_tile, face_cell, profile):
    vm = pltpu.VMEM
    dma = pltpu.SemaphoreType.DMA
    small = (FACES // NZ, NZ)
    scratch = [
        vm((2 * SPAN, NZ), f32), vm((2 * SPAN, NZ), f32), vm((SPAN, NZ), f32), vm((FACES, NZ), f32),
        vm((SLOTS, NZ), f32), vm((SLOTS, NZ), f32),
        vm((GROUPS, 8, NZ), f32), vm((GROUPS, 8, NZ), f32),
        vm(small, i32), vm(small, i32), vm((14 * GROUPS, FACES), bf16), vm((NZ, FACES), bf16),
        vm((2 * GROUPS, NZ), f32), vm((2 * GROUPS, NZ), f32),
        vm((2 * GROUPS, NZ), i32), pltpu.SMEM((2 * GROUPS, NZ), i32),
        vm((2 * GROUPS, NZ), i32), pltpu.SMEM((2 * GROUPS, NZ), i32),
        vm((4 * CELLS + 8, NZ), f32), vm((4 * CAP + 8, NZ), f32), vm((5 * GROUPS, 8, NZ), f32),
        vm((NZ, SLOTS), bf16), vm((SLOTS, NZ), bf16), vm((6 * GROUPS, 8 * NZ), bf16), vm((2 * GROUPS, NZ), f32),
        vm((6, CELLS + CY, NZ), f32), vm((2 * GROUPS, NZ), i32),
        vm((2, 3 * CY, NZ), f32), vm((2, 3 * CX, NZ), f32), vm((2, 2 * CY, NZ), f32), vm((2, 2 * CX, NZ), f32),
        vm((2, 3 * CY, NZ), f32), vm((2, 3 * CX, NZ), f32), vm((2, 2 * CY, NZ), f32), vm((2, 2 * CX, NZ), f32),
        vm((GROUPS, 8, NZ), f32), vm((GROUPS, 8, NZ), f32),
        vm(small, f32), vm(small, i32), vm(small, i32), vm((1, NZ), f32),
        dma((8,)), dma((2,)), dma((GROUPS,)), dma((GROUPS,)), dma((GROUPS,)), dma((GROUPS,)),
        dma((8,)), dma((8,)), dma((GROUPS,)), dma((GROUPS,)),
    ]
    whole = pl.BlockSpec(memory_space=pltpu.HBM)
    inside = pl.BlockSpec(memory_space=pltpu.VMEM)
    out, stress = pl.pallas_call(
        kernel,
        out_shape=(
            jax.ShapeDtypeStruct((2 * CELLS, NZ), f32),
            jax.ShapeDtypeStruct((2, FACES), f32),
        ),
        in_specs=[whole] * 7,
        out_specs=(inside, inside),
        scratch_shapes=scratch,
        compiler_params=pltpu.CompilerParams(
            collective_id=0, has_side_effects=True, vmem_limit_bytes=48 * 1024 * 1024
        ),
    )(*[pltpu.with_memory_space_constraint(array, pltpu.HBM) for array in (
        velocity.reshape(2 * CELLS, NZ), metric.reshape(CELLS, NZ), weights,
        reynolds.reshape(small), face_tile.reshape(small), face_cell.reshape(small), profile.reshape(1, NZ),
    )])
    return out.reshape(2, CX, CY, NZ), stress


def solution(mesh):
    placed = (
        P(None, "gx", "gy", None),
        P("gx", "gy", None),
        P(("gx", "gy"), None),
        P(("gx", "gy")),
        P(("gx", "gy"), None),
        P(("gx", "gy")),
        P(),
    )
    return jax.shard_map(
        local,
        mesh=mesh,
        in_specs=placed,
        out_specs=(P(None, "gx", "gy", None), P(None, ("gx", "gy"))),
        check_vma=False,
    )
```

```python
import jax
import jax.numpy as jnp
from jax import lax
from jax.experimental import pallas as pl
from jax.experimental.pallas import tpu as pltpu
from jax.sharding import PartitionSpec as P

WALL_ITERS = 3
CAP = 256
CX = 64
CY = 32
NZ = 128
FACES = 2048
SIDE = 4
GROUPS = SIDE * SIDE
SLOTS = GROUPS * CAP
CELLS = CX * CY
SPAN = (CX + 2) * CY
BLOCK = CAP // 8
RUN = 4
PIECES = 4

karman = 0.41
time_step = 0.2
viscosity = 0.5

MESH = pl.DeviceIdType.MESH
f32 = jnp.float32
bf16 = jnp.bfloat16
i32 = jnp.int32

NT = (((1,), (1,)), ((), ()))

ORDER = (0, 10, 4, 12, 1, 3, 6, 14, 9, 11, 8, 2, 5, 15, 7, 13)


def iota(shape, dim):
    return lax.broadcasted_iota(i32, shape, dim)


def mm(a, b):
    return jnp.dot(a, b, preferred_element_type=f32)


def mm_nt(a, b):
    return lax.dot_general(a, b, NT, preferred_element_type=f32)


def thirds(value):
    first = value.astype(bf16)
    rest = value - first.astype(f32)
    second = rest.astype(bf16)
    third = (rest - second.astype(f32)).astype(bf16)
    return first, second, third


def nth(index):
    words = [sum(step << (4 * k) for k, step in enumerate(ORDER[h : h + 4])) for h in (0, 4, 8, 12)]
    word = jnp.where(index < 8, jnp.where(index < 4, words[0], words[1]), jnp.where(index < 12, words[2], words[3]))
    return (word >> (4 * (index % 4))) & 15


def wall_stress(m0, m1, reynolds):
    speed = jnp.sqrt(m0 * m0 + m1 * m1 + 1.0)
    friction = 0.05 * speed
    for sweep in range(WALL_ITERS):
        friction = karman * speed / jnp.log(9.0 + reynolds * friction)
    factor = friction * friction / speed
    return factor * m0, factor * m1


def kernel(
    vel, met, wgt, rey_in, tile_in, cell_in, prof_in,
    out, stress_out,
    v0, v1, jac, win, wsend, wrecv, msend, mrecv, lo_face, hi_face, a_face, b_face,
    meta_cell, meta_rey, cell_v, cell_s, inv_v, inv_s, cols, picked, dots, b_slot, b_rows, a_slot, so_far, factors, slot_hi,
    hx, hy, hx2, hy2, ex, ey, ex2, ey2, rsend, rrecv,
    rey_ref, tile_ref, cell_ref, prof_ref,
    in_sem, smem_sem, ms_sem, mr_sem, ws_sem, wr_sem, hs_sem, hr_sem, rs_sem, rr_sem,
):
    gx = lax.axis_index("gx")
    gy = lax.axis_index("gy")
    mz = gy // SIDE
    mx = gy % SIDE

    def peer(step):
        return ((mz + step // SIDE) % SIDE) * SIDE + (mx + step % SIDE) % SIDE

    def target(index):
        return peer(ORDER[index] if isinstance(index, int) else nth(index))

    def origin(index):
        step = ORDER[index]
        return peer(((SIDE - step // SIDE) % SIDE) * SIDE + (SIDE - step % SIDE) % SIDE)

    n_gx = lax.axis_size("gx")
    east = (lax.rem(gx + 1, n_gx), gy)
    west = (lax.rem(gx + n_gx - 1, n_gx), gy)
    north = (gx, lax.rem(gy + 1, GROUPS))
    south = (gx, lax.rem(gy + GROUPS - 1, GROUPS))

    barrier = pltpu.get_barrier_semaphore()
    for step in range(1, GROUPS):
        pl.semaphore_signal(barrier, inc=1, device_id=(gx, peer(step)), device_id_type=MESH)
    for side in (east, west):
        pl.semaphore_signal(barrier, inc=1, device_id=side, device_id_type=MESH)

    small_in = [
        pltpu.make_async_copy(tile_in, tile_ref, in_sem.at[4]),
        pltpu.make_async_copy(cell_in, cell_ref, in_sem.at[5]),
        pltpu.make_async_copy(rey_in, rey_ref, in_sem.at[6]),
        pltpu.make_async_copy(prof_in, prof_ref, in_sem.at[7]),
    ]
    for copy in small_in:
        copy.start()
    loads_in = [
        pltpu.make_async_copy(wgt, win, in_sem.at[0]),
        pltpu.make_async_copy(vel.at[pl.ds(0, CELLS)], v0.at[pl.ds(CY, CELLS)], in_sem.at[1]),
        pltpu.make_async_copy(vel.at[pl.ds(CELLS, CELLS)], v0.at[pl.ds(SPAN + CY, CELLS)], in_sem.at[2]),
        pltpu.make_async_copy(met, jac.at[pl.ds(CY, CELLS)], in_sem.at[3]),
    ]
    for copy in loads_in:
        copy.start()

    for copy in small_in:
        copy.wait()
    chunks = FACES // NZ
    tile = tile_ref[...]
    away = (((tile // SIDE) - mz + SIDE) % SIDE) * SIDE + ((tile % SIDE) - mx + SIDE) % SIDE
    member = jnp.concatenate([(away == step).astype(f32) for step in ORDER], axis=0)
    member16 = member.astype(bf16)
    upto = (iota((NZ, NZ), 0) <= iota((NZ, NZ), 1)).astype(f32).astype(bf16)
    rows_i = iota((GROUPS * chunks, GROUPS * chunks), 0)
    cols_i = iota((GROUPS * chunks, GROUPS * chunks), 1)
    ahead = ((rows_i // chunks == cols_i // chunks) & (cols_i < rows_i)).astype(f32).astype(bf16)
    ones = jnp.ones((2 * NZ, NZ), bf16)
    earlier = mm(mm(ahead, member16).astype(bf16), ones[:NZ])
    rank = mm(member16, upto) + earlier
    order = jnp.zeros((chunks, NZ), f32)
    chunk_of = jnp.zeros((chunks, NZ), f32)
    for t in range(GROUPS):
        sl = slice(t * chunks, (t + 1) * chunks)
        order = order + member[sl] * rank[sl]
        chunk_of = chunk_of + member[sl] * float(t)
    order = order.astype(i32) - 1
    chunk_of = chunk_of.astype(i32)
    hi = (chunk_of // SIDE) * 8 + order % 8
    lo = (chunk_of % SIDE) * BLOCK + order // 8
    hi_face[...] = hi
    lo_face[...] = lo
    cell = cell_ref[...]
    cell_hi = (cell // NZ + 1).astype(f32)
    cell_lo = (cell % NZ).astype(f32)
    r1, r2, r3 = thirds(rey_ref[...])
    r1, r2, r3 = r1.astype(f32), r2.astype(f32), r3.astype(f32)
    lane_row = iota((1, NZ), 1).astype(f32)
    for ch in range(chunks):
        one = slice(ch, ch + 1)
        span = slice(ch * NZ, (ch + 1) * NZ)
        b_face[:, span] = (iota((NZ, NZ), 0) == lo[one]).astype(f32).astype(bf16)
        mask = iota((2 * GROUPS, NZ), 0) == hi[one]
        values = [
            jnp.full((1, NZ), float(ch), f32), lane_row, cell_hi[one], cell_lo[one], r1[one], r2[one], r3[one],
        ]
        a_face[:, span] = jnp.concatenate([jnp.where(mask, v, 0.0) for v in values], axis=0).astype(bf16)
    table = mm_nt(a_face[...], b_face[...])
    part = [table[q * 2 * GROUPS : (q + 1) * 2 * GROUPS] for q in range(7)]
    inv_v[...] = jnp.clip((part[0] * float(NZ) + part[1]).astype(i32), 0, FACES - 1)
    slot_cell = jnp.where(part[2] > 0.0, (part[2] - 1.0) * float(NZ) + part[3], -1.0)
    slot_rey = (part[4] + part[5]) + part[6]
    to_smem = pltpu.make_async_copy(inv_v, inv_s, smem_sem.at[0])
    to_smem.start()
    lanes8 = iota((8, NZ), 1) // BLOCK
    for g in range(SIDE):
        eight = slice(g * 8, (g + 1) * 8)
        beside = pltpu.roll(slot_rey[eight], BLOCK, 1)
        for k in range(SIDE):
            msend[g * SIDE + k] = jnp.where(lanes8 == k, slot_cell[eight], beside)

    def meta_copy(step):
        return pltpu.make_async_remote_copy(
            src_ref=msend.at[step], dst_ref=mrecv.at[step],
            send_sem=ms_sem.at[step], recv_sem=mr_sem.at[step],
            device_id=(gx, target(step)), device_id_type=MESH,
        )

    def weight_copy(step):
        return pltpu.make_async_remote_copy(
            src_ref=wsend.at[pl.ds(step * CAP, CAP)], dst_ref=wrecv.at[pl.ds(step * CAP, CAP)],
            send_sem=ws_sem.at[step], recv_sem=wr_sem.at[step],
            device_id=(gx, target(step)), device_id_type=MESH,
        )

    def stress_copy(step):
        return pltpu.make_async_remote_copy(
            src_ref=rsend.at[step], dst_ref=rrecv.at[step],
            send_sem=rs_sem.at[step], recv_sem=rr_sem.at[step],
            device_id=(gx, origin(step)),
            device_id_type=MESH,
        )

    def gather(table, step, source, rows, target, first):
        where = table.at[pl.ds((step // SIDE) * 8, 8), pl.ds((step % SIDE) * BLOCK, BLOCK)]
        for v in range(0, BLOCK, 4):
            places = [(k % 8, v + k // 8) for k in range(32)]
            runs = [source[pl.ds(where[place], rows), :] for place in places]
            for k, run in enumerate(runs):
                target[pl.ds(first + (v * 8 + k) * rows, rows), :] = run

    to_smem.wait()
    loads_in[0].wait()
    gather(inv_s, 1, win, 1, wsend, CAP)

    pl.semaphore_wait(barrier, GROUPS + 1)
    weight_copy(1).start()


    def edges(buffer, jacobian, x_edge, y_edge):
        for n, at in enumerate((CY, CX * CY)):
            for c in range(2):
                x_edge[n, pl.ds(c * CY, CY), :] = buffer[pl.ds(c * SPAN + at, CY), :]
            if jacobian is not None:
                x_edge[n, pl.ds(2 * CY, CY), :] = jacobian[pl.ds(at, CY), :]
        for n, at in enumerate((CY, CY + CY - 1)):
            for c in range(2):
                y_edge[n, pl.ds(c * CX, CX), :] = buffer[pl.ds(c * SPAN + at, CX, stride=CY), :]
            if jacobian is not None:
                y_edge[n, pl.ds(2 * CX, CX), :] = jacobian[pl.ds(at, CX, stride=CY), :]

    def halo_copies(x_edge, y_edge, x_halo, y_halo, base):
        made = []
        for n, (edge, halo, way, device) in enumerate((
            (x_edge, x_halo, 0, west), (x_edge, x_halo, 1, east),
            (y_edge, y_halo, 0, south), (y_edge, y_halo, 1, north),
        )):
            made.append(pltpu.make_async_remote_copy(
                src_ref=edge.at[way], dst_ref=halo.at[way],
                send_sem=hs_sem.at[base + n], recv_sem=hr_sem.at[base + n],
                device_id=device, device_id_type=MESH,
            ))
        return made

    halos = halo_copies(ex, ey, hx, hy, 0)

    def pack_send(step, carry):
        gather(inv_s, step, win, 1, wsend, step * CAP)
        weight_copy(step).start()

        @pl.when(step == 3)
        def _():
            for other in range(1, GROUPS):
                meta_copy(other).start()

        @pl.when(step == 4)
        def _():
            for copy in loads_in[1:]:
                copy.wait()
            edges(v0, jac, ex, ey)
            for copy in halos:
                copy.start()

        return carry

    lax.fori_loop(2, GROUPS, pack_send, 0)
    gather(inv_s, 0, win, 1, wrecv, 0)

    for step in range(1, GROUPS):
        meta_copy(step).wait_recv()

    def four(first, received, g):
        tiles = [first if g + k == 0 else received[g * SIDE + k] for k in range(SIDE)]
        rows, others = tiles[0], tiles[SIDE - 1]
        for k in range(1, SIDE):
            rows = jnp.where(lanes8 == k, tiles[k], rows)
            others = jnp.where(lanes8 == k, tiles[k - 1], others)
        return rows, pltpu.roll(others, NZ - BLOCK, 1)

    for g in range(SIDE):
        rows, others = four(msend[0], mrecv, g)
        meta_cell[g * 8 : (g + 1) * 8, :] = rows
        meta_rey[g * 8 : (g + 1) * 8, :] = others
    slot_of = meta_cell[...].astype(i32)
    cell_v[...] = jnp.clip(slot_of, 0, CELLS - 1) * 4
    cells_smem = pltpu.make_async_copy(cell_v, cell_s, smem_sem.at[1])
    cells_smem.start()
    used = slot_of >= 0
    s_hi = jnp.where(used, slot_of // NZ, -1)
    slot_hi[...] = s_hi
    s_lo = jnp.where(used, slot_of % NZ, -1)
    for j in range(2 * GROUPS):
        seen = (iota((NZ, NZ), 0) == s_lo[j : j + 1]).astype(f32)
        b_slot[:, j * NZ : (j + 1) * NZ] = seen.astype(bf16)
        b_rows[j * NZ : (j + 1) * NZ, :] = jnp.transpose(seen).astype(bf16)

    for copy in halos:
        copy.wait_recv()

    row_y = iota((CY, NZ), 0)
    lane = iota((CY, NZ), 1)
    at_first, at_last = row_y == 0, row_y == CY - 1

    for c in range(2):
        v0[pl.ds(c * SPAN + (CX + 1) * CY, CY), :] = hx[0, pl.ds(c * CY, CY), :]
        v0[pl.ds(c * SPAN, CY), :] = hx[1, pl.ds(c * CY, CY), :]
    jac[pl.ds((CX + 1) * CY, CY), :] = hx[0, pl.ds(2 * CY, CY), :]
    jac[pl.ds(0, CY), :] = hx[1, pl.ds(2 * CY, CY), :]

    def star(buffer, base, halo, row, x):
        at = pl.multiple_of(base + (x + 1) * CY, CY)
        centre = buffer[pl.ds(at, CY), :]
        next_x = buffer[pl.ds(pl.multiple_of(at + CY, CY), CY), :]
        last_x = buffer[pl.ds(pl.multiple_of(at - CY, CY), CY), :]
        next_y = buffer[pl.ds(at + 1, CY), :]
        last_y = buffer[pl.ds(at - 1, CY), :]
        next_y = jnp.where(at_last, halo[0, pl.ds(row + x, 1), :], next_y)
        last_y = jnp.where(at_first, halo[1, pl.ds(row + x, 1), :], last_y)
        return centre, next_x, last_x, next_y, last_y

    def column_sum(v, level):
        above = jnp.where(level == NZ - 1, 0.0, pltpu.roll(v, NZ - 1, 1))
        below = jnp.where(level == 0, 0.0, pltpu.roll(v, 1, 1))
        return above + below

    def first_step(x, carry):
        j, j_e, j_w, j_n, j_s = star(jac, 0, hy, 2 * CX, x)
        inverse = 1.0 / j
        k_h = (time_step * viscosity * 0.5) * inverse
        k_v = (time_step * viscosity) * inverse * inverse
        k_e, k_w, k_n, k_s = k_h * (j + j_e), k_h * (j + j_w), k_h * (j + j_n), k_h * (j + j_s)
        k_c = (k_e + k_w) + (k_n + k_s) + 2.0 * k_v
        at = pl.ds(pl.multiple_of(x * CY, CY), CY)
        for n, k in enumerate((k_e, k_w, k_n, k_s, k_v, k_c)):
            factors[n, at, :] = k
        stars = [star(v0, c * SPAN, hy, c * CX, x) for c in range(2)]
        along = (-0.5 * time_step) * stars[0][0]
        across = (-0.5 * time_step) * stars[1][0]
        k_e, k_w, k_n, k_s = k_e + along, k_w - along, k_n + across, k_s - across
        for c in range(2):
            v, e, w, n, s = stars[c]
            new = v + ((k_e * e + k_w * w) + (k_n * n + k_s * s) + (k_v * column_sum(v, lane) - k_c * v))
            v1[pl.ds(pl.multiple_of(c * SPAN + (x + 1) * CY, CY), CY), :] = new
            cols[pl.ds(x * (4 * CY) + c, CY, stride=4), :] = v
            cols[pl.ds(x * (4 * CY) + 2 + c, CY, stride=4), :] = new
        return carry

    tall = RUN * CY
    y_tall, lane_tall = iota((tall, NZ), 0) % CY, iota((tall, NZ), 1)

    def second_step(run, carry):
        x = run * RUN
        at = pl.ds(pl.multiple_of(x * CY, tall), tall)
        k_e, k_w, k_n, k_s, k_v, k_c = [factors[n, at, :] for n in range(6)]
        here = [pl.multiple_of(c * SPAN + (x + 1) * CY, CY) for c in range(2)]
        centre = [v1[pl.ds(here[c], tall), :] for c in range(2)]
        along = (-0.5 * time_step) * centre[0]
        across = (-0.5 * time_step) * centre[1]
        k_e, k_w = k_e + along, k_w - along
        k_n = jnp.where(y_tall == CY - 1, 0.0, k_n + across)
        k_s = jnp.where(y_tall == 0, 0.0, k_s - across)
        for c in range(2):
            v = centre[c]
            e = v1[pl.ds(pl.multiple_of(here[c] + CY, CY), tall), :]
            w = v1[pl.ds(pl.multiple_of(here[c] - CY, CY), tall), :]
            n = v1[pl.ds(here[c] + 1, tall), :]
            s = v1[pl.ds(here[c] - 1, tall), :]
            change = (k_e * e + k_w * w) + (k_n * n + k_s * s) + (k_v * column_sum(v, lane_tall) - k_c * v)
            at = pl.ds(pl.multiple_of(c * CELLS + x * CY, tall), tall)
            out[at, :] = out[at, :] + change
        return carry

    def first_pair(pair, carry):
        return first_step(2 * pair + 1, first_step(2 * pair, carry))

    lax.fori_loop(0, CX // 2, first_pair, 0)

    cells_smem.wait()
    profile = prof_ref[...]

    lane8 = iota((8, NZ), 1) % BLOCK

    def chunk(step):
        gather(cell_s, step, cols, 4, picked, 0)
        weights = wrecv[pl.ds(pl.multiple_of(step * CAP, CAP), CAP), :]
        for q in range(5):
            if q < 4:
                product = picked[pl.ds(q, CAP, stride=4), :] * weights
            else:
                product = weights * profile
            total = jnp.sum(product, axis=1, keepdims=True)
            rows = jnp.zeros((8, NZ), f32)
            for v in range(BLOCK):
                rows = jnp.where(lane8 == v, total[v * 8 : (v + 1) * 8], rows)
            dots[pl.ds(q * GROUPS + step, 1)] = rows.reshape(1, 8, NZ)

    def arrived(step, carry):
        @pl.when(step > 0)
        def _():
            weight_copy(step).wait_recv()

        chunk(step)
        return carry

    def group_sums(q, g):
        rows = dots[q * GROUPS + g * SIDE]
        for k in range(1, SIDE):
            rows = jnp.where(lanes8 == k, dots[q * GROUPS + g * SIDE + k], rows)
        return rows

    def eight_rows(ref, g):
        return ref[pl.ds(g * 8 if isinstance(g, int) else pl.multiple_of(g * 8, 8), 8), :]

    def group_load(stress, g):
        high = eight_rows(slot_hi, g)
        pieces = [[p.astype(f32) for p in thirds(jnp.where(high >= 0, s, 0.0))] for s in stress]
        for sub in range(8):
            one = slice(sub, sub + 1)
            mask = iota((GROUPS, NZ), 0) == high[one]
            parts = [jnp.where(mask, pieces[c][k][one], 0.0) for k in range(3) for c in range(2)]
            a_slot[g, :, sub * NZ : (sub + 1) * NZ] = jnp.concatenate(parts, axis=0).astype(bf16)
        total = mm(a_slot[g], b_rows[pl.ds((g * 8 * NZ if isinstance(g, int) else pl.multiple_of(g * 8 * NZ, 8 * NZ)), 8 * NZ), :])
        width = 2 * GROUPS
        so_far[...] = so_far[...] + ((total[0:width] + total[width : 2 * width]) + total[2 * width : 3 * width])

    def by_cell(load):
        return jnp.transpose(jnp.concatenate([load, jnp.zeros((NZ - 2 * GROUPS, NZ), f32)], axis=0))

    def group(g, carry):
        lax.fori_loop(g * SIDE, (g + 1) * SIDE, arrived, 0)
        group_load(wall_stress(group_sums(0, g), group_sums(1, g), eight_rows(meta_rey, g)), g)
        return carry

    so_far[...] = jnp.zeros((2 * GROUPS, NZ), f32)
    lax.fori_loop(0, SIDE, group, 0)
    load = so_far[...]

    spread = by_cell(load)
    for c in range(2):
        for block in range(CELLS // NZ):
            at = pl.ds(c * SPAN + CY + block * NZ, NZ)
            column = c * GROUPS + block
            v1[at, :] = v1[at, :] - spread[:, column : column + 1] * profile

    edges(v1, None, ex2, ey2)
    halos2 = halo_copies(ex2, ey2, hx2, hy2, 4)
    for copy in halos2:
        copy.start()

    pieces = jnp.concatenate(thirds(load), axis=0)
    width = 2 * GROUPS
    so_far[...] = jnp.zeros((2 * GROUPS, NZ), f32)

    def second_group(g, carry):
        high = eight_rows(slot_hi, g)
        seen = mm(pieces, b_slot[:, pl.ds((g * 8 * NZ if isinstance(g, int) else pl.multiple_of(g * 8 * NZ, 8 * NZ)), 8 * NZ)])
        seen = (seen[0:width] + seen[width : 2 * width]) + seen[2 * width : 3 * width]
        met_load = [[], []]
        for sub in range(8):
            mask = iota((GROUPS, NZ), 0) == high[sub : sub + 1]
            for c in range(2):
                at_face = jnp.where(mask, seen[c * GROUPS : (c + 1) * GROUPS, sub * NZ : (sub + 1) * NZ], 0.0)
                met_load[c].append(jnp.sum(at_face, axis=0, keepdims=True))
        met_load = [jnp.concatenate(rows, axis=0) for rows in met_load]
        shape = group_sums(4, g)
        stress = wall_stress(
            group_sums(2, g) - met_load[0] * shape, group_sums(3, g) - met_load[1] * shape, eight_rows(meta_rey, g)
        )
        beside = pltpu.roll(stress[1], BLOCK, 1)
        for k in range(SIDE):
            rsend[g * SIDE + k] = jnp.where(lanes8 == k, stress[0], beside)
        return stress

    stresses = [second_group(g, 0) for g in range(SIDE)]
    for step in range(1, GROUPS):
        stress_copy(step).start()
    for g in range(SIDE):
        group_load(stresses[g], g)

    load = so_far[...]
    spread = by_cell(load)
    for c in range(2):
        for block in range(CELLS // NZ):
            at = pl.ds(c * SPAN + CY + block * NZ, NZ)
            column = c * GROUPS + block
            out[pl.ds(c * CELLS + block * NZ, NZ), :] = v1[at, :] - spread[:, column : column + 1] * profile

    lax.fori_loop(1, CX // RUN - 1, second_step, 0)
    for copy in halos:
        copy.wait_send()
    for step in range(1, GROUPS):
        meta_copy(step).wait_send()
        weight_copy(step).wait_send()
    for copy in halos2:
        copy.wait_recv()
    for c in range(2):
        v1[pl.ds(c * SPAN + (CX + 1) * CY, CY), :] = hx2[0, pl.ds(c * CY, CY), :]
        v1[pl.ds(c * SPAN, CY), :] = hx2[1, pl.ds(c * CY, CY), :]
    lax.fori_loop(0, 2, lambda n, carry: second_step(n * (CX // RUN - 1), carry), 0)
    for side, row, sign in ((0, CY - 1, 1.0), (1, 0, -1.0)):
        factor = factors[2 + side, pl.ds(row, CX, stride=CY), :]
        factor = factor + (sign * -0.5 * time_step) * v1[pl.ds(SPAN + CY + row, CX, stride=CY), :]
        for c in range(2):
            added = hy2[side, pl.ds(c * CX, CX), :] * factor
            most = CX - 8
            at = pl.ds(c * CELLS + row, most, stride=CY)
            out[at, :] = out[at, :] + added[:most]
            for x in range(most, CX):
                at = pl.ds(c * CELLS + row + x * CY, 1)
                out[at, :] = out[at, :] + added[x : x + 1]

    for step in range(1, GROUPS):
        stress_copy(step).wait_recv()
    back = jnp.concatenate([rows for g in range(SIDE) for rows in four(rsend[0], rrecv, g)], axis=0)
    pieces = jnp.concatenate(thirds(back), axis=0)
    width = SIDE * 16
    for ch in range(chunks):
        one = slice(ch, ch + 1)
        span = slice(ch * NZ, (ch + 1) * NZ)
        seen = b_face[:, span]
        spread = mm(pieces, seen)
        spread = (spread[0:width] + spread[width : 2 * width]) + spread[2 * width : 3 * width]
        place = hi_face[one, :]
        row = (place // 8) * 16 + place % 8
        for c in range(2):
            mask = iota((SIDE * 16, NZ), 0) == row + c * 8
            stress_out[c : c + 1, span] = jnp.sum(jnp.where(mask, spread, 0.0), axis=0, keepdims=True)

    for copy in halos2:
        copy.wait_send()
    for step in range(1, GROUPS):
        stress_copy(step).wait_send()


def write_out(velocity, stress, velocity_out, stress_out, sem):
    rows = 2 * CELLS // PIECES
    copies = [pltpu.make_async_copy(stress, stress_out, sem.at[PIECES])]
    for n in range(PIECES):
        part = pl.ds(n * rows, rows)
        copies.append(pltpu.make_async_copy(velocity.at[part], velocity_out.at[part], sem.at[n]))
    for copy in copies:
        copy.start()
    for copy in copies:
        copy.wait()


def local(velocity, metric, weights, reynolds, face_tile, face_cell, profile):
    vm = pltpu.VMEM
    dma = pltpu.SemaphoreType.DMA
    small = (FACES // NZ, NZ)
    scratch = [
        vm((2 * SPAN, NZ), f32), vm((2 * SPAN, NZ), f32), vm((SPAN, NZ), f32), vm((FACES, NZ), f32),
        vm((SLOTS, NZ), f32), vm((SLOTS, NZ), f32),
        vm((GROUPS, 8, NZ), f32), vm((GROUPS, 8, NZ), f32),
        vm(small, i32), vm(small, i32), vm((14 * GROUPS, FACES), bf16), vm((NZ, FACES), bf16),
        vm((2 * GROUPS, NZ), f32), vm((2 * GROUPS, NZ), f32),
        vm((2 * GROUPS, NZ), i32), pltpu.SMEM((2 * GROUPS, NZ), i32),
        vm((2 * GROUPS, NZ), i32), pltpu.SMEM((2 * GROUPS, NZ), i32),
        vm((4 * CELLS + 8, NZ), f32), vm((4 * CAP + 8, NZ), f32), vm((5 * GROUPS, 8, NZ), f32),
        vm((NZ, SLOTS), bf16), vm((SLOTS, NZ), bf16), vm((SIDE, 6 * GROUPS, 8 * NZ), bf16), vm((2 * GROUPS, NZ), f32),
        vm((6, CELLS + CY, NZ), f32), vm((2 * GROUPS, NZ), i32),
        vm((2, 3 * CY, NZ), f32), vm((2, 3 * CX, NZ), f32), vm((2, 2 * CY, NZ), f32), vm((2, 2 * CX, NZ), f32),
        vm((2, 3 * CY, NZ), f32), vm((2, 3 * CX, NZ), f32), vm((2, 2 * CY, NZ), f32), vm((2, 2 * CX, NZ), f32),
        vm((GROUPS, 8, NZ), f32), vm((GROUPS, 8, NZ), f32),
        vm(small, f32), vm(small, i32), vm(small, i32), vm((1, NZ), f32),
        dma((8,)), dma((2,)), dma((GROUPS,)), dma((GROUPS,)), dma((GROUPS,)), dma((GROUPS,)),
        dma((8,)), dma((8,)), dma((GROUPS,)), dma((GROUPS,)),
    ]
    whole = pl.BlockSpec(memory_space=pltpu.HBM)
    inside = pl.BlockSpec(memory_space=pltpu.VMEM)
    out, stress = pl.pallas_call(
        kernel,
        out_shape=(
            pltpu.VMEM((2 * CELLS, NZ), f32),
            pltpu.VMEM((2, FACES), f32),
        ),
        in_specs=[whole] * 7,
        out_specs=(inside, inside),
        scratch_shapes=scratch,
        compiler_params=pltpu.CompilerParams(
            collective_id=0, has_side_effects=True, vmem_limit_bytes=48 * 1024 * 1024
        ),
    )(*[pltpu.with_memory_space_constraint(array, pltpu.HBM) for array in (
        velocity.reshape(2 * CELLS, NZ), metric.reshape(CELLS, NZ), weights,
        reynolds.reshape(small), face_tile.reshape(small), face_cell.reshape(small), profile.reshape(1, NZ),
    )])
    out, stress = pl.pallas_call(
        write_out,
        out_shape=(
            jax.ShapeDtypeStruct((2 * CELLS, NZ), f32),
            jax.ShapeDtypeStruct((2, FACES), f32),
        ),
        in_specs=[inside, inside],
        out_specs=(whole, whole),
        scratch_shapes=[dma((PIECES + 1,))],
        compiler_params=pltpu.CompilerParams(vmem_limit_bytes=4 * 1024 * 1024),
    )(*[pltpu.with_memory_space_constraint(array, pltpu.VMEM) for array in (out, stress)])
    return out.reshape(2, CX, CY, NZ), stress


def solution(mesh):
    placed = (
        P(None, "gx", "gy", None),
        P("gx", "gy", None),
        P(("gx", "gy"), None),
        P(("gx", "gy")),
        P(("gx", "gy"), None),
        P(("gx", "gy")),
        P(),
    )
    return jax.shard_map(
        local,
        mesh=mesh,
        in_specs=placed,
        out_specs=(P(None, "gx", "gy", None), P(None, ("gx", "gy"))),
        check_vma=False,
    )
```

```python
import jax
import jax.numpy as jnp
from jax import lax
from jax.experimental import pallas as pl
from jax.experimental.pallas import tpu as pltpu
from jax.sharding import PartitionSpec as P

WALL_ITERS = 3
CAP = 256
CX = 64
CY = 32
NZ = 128
FACES = 2048
SIDE = 4
GROUPS = SIDE * SIDE
SLOTS = GROUPS * CAP
CELLS = CX * CY
SPAN = (CX + 2) * CY
BLOCK = CAP // 8
RUN = 4
PIECES = 4

karman = 0.41
time_step = 0.2
viscosity = 0.5

MESH = pl.DeviceIdType.MESH
f32 = jnp.float32
bf16 = jnp.bfloat16
i32 = jnp.int32

NT = (((1,), (1,)), ((), ()))

ORDER = (0, 10, 4, 12, 1, 3, 6, 14, 9, 11, 8, 2, 5, 15, 7, 13)


def iota(shape, dim):
    return lax.broadcasted_iota(i32, shape, dim)


def mm(a, b):
    return jnp.dot(a, b, preferred_element_type=f32)


def mm_nt(a, b):
    return lax.dot_general(a, b, NT, preferred_element_type=f32)


def thirds(value):
    first = value.astype(bf16)
    rest = value - first.astype(f32)
    second = rest.astype(bf16)
    third = (rest - second.astype(f32)).astype(bf16)
    return first, second, third


def nth(index):
    words = [sum(step << (4 * k) for k, step in enumerate(ORDER[h : h + 4])) for h in (0, 4, 8, 12)]
    word = jnp.where(index < 8, jnp.where(index < 4, words[0], words[1]), jnp.where(index < 12, words[2], words[3]))
    return (word >> (4 * (index % 4))) & 15


def wall_stress(m0, m1, reynolds):
    speed = jnp.sqrt(m0 * m0 + m1 * m1 + 1.0)
    friction = 0.05 * speed
    for sweep in range(WALL_ITERS):
        friction = karman * speed / jnp.log(9.0 + reynolds * friction)
    factor = friction * friction / speed
    return factor * m0, factor * m1


def kernel(
    vel, met, wgt, rey_in, tile_in, cell_in, prof_in,
    out, stress_out,
    v0, v1, jac, win, wsend, wrecv, msend, mrecv, lo_face, hi_face, a_face, b_face,
    meta_cell, meta_rey, cell_v, cell_s, inv_v, inv_s, cols, picked, dots, b_slot, b_rows, a_slot, so_far, factors, slot_hi,
    hx, hy, hx2, hy2, ex, ey, ex2, ey2, rsend, rrecv,
    rey_ref, tile_ref, cell_ref, prof_ref,
    in_sem, smem_sem, ms_sem, mr_sem, ws_sem, wr_sem, hs_sem, hr_sem, rs_sem, rr_sem,
):
    gx = lax.axis_index("gx")
    gy = lax.axis_index("gy")
    mz = gy // SIDE
    mx = gy % SIDE

    def peer(step):
        return ((mz + step // SIDE) % SIDE) * SIDE + (mx + step % SIDE) % SIDE

    def target(index):
        return peer(ORDER[index] if isinstance(index, int) else nth(index))

    def origin(index):
        step = ORDER[index]
        return peer(((SIDE - step // SIDE) % SIDE) * SIDE + (SIDE - step % SIDE) % SIDE)

    n_gx = lax.axis_size("gx")
    east = (lax.rem(gx + 1, n_gx), gy)
    west = (lax.rem(gx + n_gx - 1, n_gx), gy)
    north = (gx, lax.rem(gy + 1, GROUPS))
    south = (gx, lax.rem(gy + GROUPS - 1, GROUPS))

    barrier = pltpu.get_barrier_semaphore()
    for step in range(1, GROUPS):
        pl.semaphore_signal(barrier, inc=1, device_id=(gx, peer(step)), device_id_type=MESH)
    for side in (east, west):
        pl.semaphore_signal(barrier, inc=1, device_id=side, device_id_type=MESH)

    small_in = [
        pltpu.make_async_copy(tile_in, tile_ref, in_sem.at[4]),
        pltpu.make_async_copy(cell_in, cell_ref, in_sem.at[5]),
        pltpu.make_async_copy(rey_in, rey_ref, in_sem.at[6]),
        pltpu.make_async_copy(prof_in, prof_ref, in_sem.at[7]),
    ]
    for copy in small_in:
        copy.start()
    loads_in = [
        pltpu.make_async_copy(wgt, win, in_sem.at[0]),
        pltpu.make_async_copy(vel.at[pl.ds(0, CELLS)], v0.at[pl.ds(CY, CELLS)], in_sem.at[1]),
        pltpu.make_async_copy(vel.at[pl.ds(CELLS, CELLS)], v0.at[pl.ds(SPAN + CY, CELLS)], in_sem.at[2]),
        pltpu.make_async_copy(met, jac.at[pl.ds(CY, CELLS)], in_sem.at[3]),
    ]
    for copy in loads_in:
        copy.start()

    for copy in small_in:
        copy.wait()
    chunks = FACES // NZ
    tile = tile_ref[...]
    away = (((tile // SIDE) - mz + SIDE) % SIDE) * SIDE + ((tile % SIDE) - mx + SIDE) % SIDE
    member = jnp.concatenate([(away == step).astype(f32) for step in ORDER], axis=0)
    member16 = member.astype(bf16)
    upto = (iota((NZ, NZ), 0) <= iota((NZ, NZ), 1)).astype(f32).astype(bf16)
    rows_i = iota((GROUPS * chunks, GROUPS * chunks), 0)
    cols_i = iota((GROUPS * chunks, GROUPS * chunks), 1)
    ahead = ((rows_i // chunks == cols_i // chunks) & (cols_i < rows_i)).astype(f32).astype(bf16)
    ones = jnp.ones((2 * NZ, NZ), bf16)
    earlier = mm(mm(ahead, member16).astype(bf16), ones[:NZ])
    rank = mm(member16, upto) + earlier
    order = jnp.zeros((chunks, NZ), f32)
    chunk_of = jnp.zeros((chunks, NZ), f32)
    for t in range(GROUPS):
        sl = slice(t * chunks, (t + 1) * chunks)
        order = order + member[sl] * rank[sl]
        chunk_of = chunk_of + member[sl] * float(t)
    order = order.astype(i32) - 1
    chunk_of = chunk_of.astype(i32)
    hi = (chunk_of // SIDE) * 8 + order % 8
    lo = (chunk_of % SIDE) * BLOCK + order // 8
    hi_face[...] = hi
    lo_face[...] = lo
    cell = cell_ref[...]
    cell_hi = (cell // NZ + 1).astype(f32)
    cell_lo = (cell % NZ).astype(f32)
    r1, r2, r3 = thirds(rey_ref[...])
    r1, r2, r3 = r1.astype(f32), r2.astype(f32), r3.astype(f32)
    lane_row = iota((1, NZ), 1).astype(f32)
    for ch in range(chunks):
        one = slice(ch, ch + 1)
        span = slice(ch * NZ, (ch + 1) * NZ)
        b_face[:, span] = (iota((NZ, NZ), 0) == lo[one]).astype(f32).astype(bf16)
        mask = iota((2 * GROUPS, NZ), 0) == hi[one]
        values = [
            jnp.full((1, NZ), float(ch), f32), lane_row, cell_hi[one], cell_lo[one], r1[one], r2[one], r3[one],
        ]
        a_face[:, span] = jnp.concatenate([jnp.where(mask, v, 0.0) for v in values], axis=0).astype(bf16)
    table = mm_nt(a_face[...], b_face[...])
    part = [table[q * 2 * GROUPS : (q + 1) * 2 * GROUPS] for q in range(7)]
    inv_v[...] = jnp.clip((part[0] * float(NZ) + part[1]).astype(i32), 0, FACES - 1)
    slot_cell = jnp.where(part[2] > 0.0, (part[2] - 1.0) * float(NZ) + part[3], -1.0)
    slot_rey = (part[4] + part[5]) + part[6]
    to_smem = pltpu.make_async_copy(inv_v, inv_s, smem_sem.at[0])
    to_smem.start()
    lanes8 = iota((8, NZ), 1) // BLOCK
    for g in range(SIDE):
        eight = slice(g * 8, (g + 1) * 8)
        beside = pltpu.roll(slot_rey[eight], BLOCK, 1)
        for k in range(SIDE):
            msend[g * SIDE + k] = jnp.where(lanes8 == k, slot_cell[eight], beside)

    def meta_copy(step):
        return pltpu.make_async_remote_copy(
            src_ref=msend.at[step], dst_ref=mrecv.at[step],
            send_sem=ms_sem.at[step], recv_sem=mr_sem.at[step],
            device_id=(gx, target(step)), device_id_type=MESH,
        )

    def weight_copy(step):
        return pltpu.make_async_remote_copy(
            src_ref=wsend.at[pl.ds(step * CAP, CAP)], dst_ref=wrecv.at[pl.ds(step * CAP, CAP)],
            send_sem=ws_sem.at[step], recv_sem=wr_sem.at[step],
            device_id=(gx, target(step)), device_id_type=MESH,
        )

    def stress_copy(step):
        return pltpu.make_async_remote_copy(
            src_ref=rsend.at[step], dst_ref=rrecv.at[step],
            send_sem=rs_sem.at[step], recv_sem=rr_sem.at[step],
            device_id=(gx, origin(step)),
            device_id_type=MESH,
        )

    def gather(table, step, source, rows, target, first):
        where = table.at[pl.ds((step // SIDE) * 8, 8), pl.ds((step % SIDE) * BLOCK, BLOCK)]
        for v in range(0, BLOCK, 4):
            places = [(k % 8, v + k // 8) for k in range(32)]
            runs = [source[pl.ds(where[place], rows), :] for place in places]
            for k, run in enumerate(runs):
                target[pl.ds(first + (v * 8 + k) * rows, rows), :] = run

    to_smem.wait()
    loads_in[0].wait()
    gather(inv_s, 1, win, 1, wsend, CAP)

    pl.semaphore_wait(barrier, GROUPS + 1)
    weight_copy(1).start()


    def edges(buffer, jacobian, x_edge, y_edge):
        for n, at in enumerate((CY, CX * CY)):
            for c in range(2):
                x_edge[n, pl.ds(c * CY, CY), :] = buffer[pl.ds(c * SPAN + at, CY), :]
            if jacobian is not None:
                x_edge[n, pl.ds(2 * CY, CY), :] = jacobian[pl.ds(at, CY), :]
        for n, at in enumerate((CY, CY + CY - 1)):
            for c in range(2):
                y_edge[n, pl.ds(c * CX, CX), :] = buffer[pl.ds(c * SPAN + at, CX, stride=CY), :]
            if jacobian is not None:
                y_edge[n, pl.ds(2 * CX, CX), :] = jacobian[pl.ds(at, CX, stride=CY), :]

    def halo_copies(x_edge, y_edge, x_halo, y_halo, base):
        made = []
        for n, (edge, halo, way, device) in enumerate((
            (x_edge, x_halo, 0, west), (x_edge, x_halo, 1, east),
            (y_edge, y_halo, 0, south), (y_edge, y_halo, 1, north),
        )):
            made.append(pltpu.make_async_remote_copy(
                src_ref=edge.at[way], dst_ref=halo.at[way],
                send_sem=hs_sem.at[base + n], recv_sem=hr_sem.at[base + n],
                device_id=device, device_id_type=MESH,
            ))
        return made

    halos = halo_copies(ex, ey, hx, hy, 0)

    def pack_send(step, carry):
        gather(inv_s, step, win, 1, wsend, step * CAP)
        weight_copy(step).start()

        @pl.when(step == 3)
        def _():
            for other in range(1, GROUPS):
                meta_copy(other).start()

        @pl.when(step == 2)
        def _():
            for copy in loads_in[1:]:
                copy.wait()
            edges(v0, jac, ex, ey)
            for copy in halos:
                copy.start()

        return carry

    lax.fori_loop(2, GROUPS, pack_send, 0)
    gather(inv_s, 0, win, 1, wrecv, 0)

    for step in range(1, GROUPS):
        meta_copy(step).wait_recv()

    def four(first, received, g):
        tiles = [first if g + k == 0 else received[g * SIDE + k] for k in range(SIDE)]
        rows, others = tiles[0], tiles[SIDE - 1]
        for k in range(1, SIDE):
            rows = jnp.where(lanes8 == k, tiles[k], rows)
            others = jnp.where(lanes8 == k, tiles[k - 1], others)
        return rows, pltpu.roll(others, NZ - BLOCK, 1)

    for g in range(SIDE):
        rows, others = four(msend[0], mrecv, g)
        meta_cell[g * 8 : (g + 1) * 8, :] = rows
        meta_rey[g * 8 : (g + 1) * 8, :] = others
    slot_of = meta_cell[...].astype(i32)
    cell_v[...] = jnp.clip(slot_of, 0, CELLS - 1) * 4
    cells_smem = pltpu.make_async_copy(cell_v, cell_s, smem_sem.at[1])
    cells_smem.start()
    used = slot_of >= 0
    s_hi = jnp.where(used, slot_of // NZ, -1)
    slot_hi[...] = s_hi
    s_lo = jnp.where(used, slot_of % NZ, -1)
    for j in range(2 * GROUPS):
        seen = (iota((NZ, NZ), 0) == s_lo[j : j + 1]).astype(f32)
        b_slot[:, j * NZ : (j + 1) * NZ] = seen.astype(bf16)
        b_rows[j * NZ : (j + 1) * NZ, :] = jnp.transpose(seen).astype(bf16)

    for copy in halos:
        copy.wait_recv()

    row_y = iota((CY, NZ), 0)
    lane = iota((CY, NZ), 1)
    at_first, at_last = row_y == 0, row_y == CY - 1

    for c in range(2):
        v0[pl.ds(c * SPAN + (CX + 1) * CY, CY), :] = hx[0, pl.ds(c * CY, CY), :]
        v0[pl.ds(c * SPAN, CY), :] = hx[1, pl.ds(c * CY, CY), :]
    jac[pl.ds((CX + 1) * CY, CY), :] = hx[0, pl.ds(2 * CY, CY), :]
    jac[pl.ds(0, CY), :] = hx[1, pl.ds(2 * CY, CY), :]

    def star(buffer, base, halo, row, x):
        at = pl.multiple_of(base + (x + 1) * CY, CY)
        centre = buffer[pl.ds(at, CY), :]
        next_x = buffer[pl.ds(pl.multiple_of(at + CY, CY), CY), :]
        last_x = buffer[pl.ds(pl.multiple_of(at - CY, CY), CY), :]
        next_y = buffer[pl.ds(at + 1, CY), :]
        last_y = buffer[pl.ds(at - 1, CY), :]
        next_y = jnp.where(at_last, halo[0, pl.ds(row + x, 1), :], next_y)
        last_y = jnp.where(at_first, halo[1, pl.ds(row + x, 1), :], last_y)
        return centre, next_x, last_x, next_y, last_y

    def column_sum(v, level):
        above = jnp.where(level == NZ - 1, 0.0, pltpu.roll(v, NZ - 1, 1))
        below = jnp.where(level == 0, 0.0, pltpu.roll(v, 1, 1))
        return above + below

    def first_step(x, carry):
        j, j_e, j_w, j_n, j_s = star(jac, 0, hy, 2 * CX, x)
        inverse = 1.0 / j
        k_h = (time_step * viscosity * 0.5) * inverse
        k_v = (time_step * viscosity) * inverse * inverse
        k_e, k_w, k_n, k_s = k_h * (j + j_e), k_h * (j + j_w), k_h * (j + j_n), k_h * (j + j_s)
        k_c = (k_e + k_w) + (k_n + k_s) + 2.0 * k_v
        at = pl.ds(pl.multiple_of(x * CY, CY), CY)
        for n, k in enumerate((k_e, k_w, k_n, k_s, k_v, k_c)):
            factors[n, at, :] = k
        stars = [star(v0, c * SPAN, hy, c * CX, x) for c in range(2)]
        along = (-0.5 * time_step) * stars[0][0]
        across = (-0.5 * time_step) * stars[1][0]
        k_e, k_w, k_n, k_s = k_e + along, k_w - along, k_n + across, k_s - across
        for c in range(2):
            v, e, w, n, s = stars[c]
            new = v + ((k_e * e + k_w * w) + (k_n * n + k_s * s) + (k_v * column_sum(v, lane) - k_c * v))
            v1[pl.ds(pl.multiple_of(c * SPAN + (x + 1) * CY, CY), CY), :] = new
            cols[pl.ds(x * (4 * CY) + c, CY, stride=4), :] = v
            cols[pl.ds(x * (4 * CY) + 2 + c, CY, stride=4), :] = new
        return carry

    tall = RUN * CY
    y_tall, lane_tall = iota((tall, NZ), 0) % CY, iota((tall, NZ), 1)

    def second_step(run, carry):
        x = run * RUN
        at = pl.ds(pl.multiple_of(x * CY, tall), tall)
        k_e, k_w, k_n, k_s, k_v, k_c = [factors[n, at, :] for n in range(6)]
        here = [pl.multiple_of(c * SPAN + (x + 1) * CY, CY) for c in range(2)]
        centre = [v1[pl.ds(here[c], tall), :] for c in range(2)]
        along = (-0.5 * time_step) * centre[0]
        across = (-0.5 * time_step) * centre[1]
        k_e, k_w = k_e + along, k_w - along
        k_n = jnp.where(y_tall == CY - 1, 0.0, k_n + across)
        k_s = jnp.where(y_tall == 0, 0.0, k_s - across)
        for c in range(2):
            v = centre[c]
            e = v1[pl.ds(pl.multiple_of(here[c] + CY, CY), tall), :]
            w = v1[pl.ds(pl.multiple_of(here[c] - CY, CY), tall), :]
            n = v1[pl.ds(here[c] + 1, tall), :]
            s = v1[pl.ds(here[c] - 1, tall), :]
            change = (k_e * e + k_w * w) + (k_n * n + k_s * s) + (k_v * column_sum(v, lane_tall) - k_c * v)
            at = pl.ds(pl.multiple_of(c * CELLS + x * CY, tall), tall)
            out[at, :] = out[at, :] + change
        return carry

    def first_pair(pair, carry):
        return first_step(2 * pair + 1, first_step(2 * pair, carry))

    lax.fori_loop(0, CX // 2, first_pair, 0)

    cells_smem.wait()
    profile = prof_ref[...]

    lane8 = iota((8, NZ), 1) % BLOCK

    def chunk(step):
        gather(cell_s, step, cols, 4, picked, 0)
        weights = wrecv[pl.ds(pl.multiple_of(step * CAP, CAP), CAP), :]
        for q in range(5):
            if q < 4:
                product = picked[pl.ds(q, CAP, stride=4), :] * weights
            else:
                product = weights * profile
            total = jnp.sum(product, axis=1, keepdims=True)
            rows = jnp.zeros((8, NZ), f32)
            for v in range(BLOCK):
                rows = jnp.where(lane8 == v, total[v * 8 : (v + 1) * 8], rows)
            dots[pl.ds(q * GROUPS + step, 1)] = rows.reshape(1, 8, NZ)

    def arrived(step, carry):
        @pl.when(step > 0)
        def _():
            weight_copy(step).wait_recv()

        chunk(step)
        return carry

    def group_sums(q, g):
        rows = dots[q * GROUPS + g * SIDE]
        for k in range(1, SIDE):
            rows = jnp.where(lanes8 == k, dots[q * GROUPS + g * SIDE + k], rows)
        return rows

    def eight_rows(ref, g):
        return ref[pl.ds(g * 8 if isinstance(g, int) else pl.multiple_of(g * 8, 8), 8), :]

    def group_load(stress, g):
        high = eight_rows(slot_hi, g)
        pieces = [[p.astype(f32) for p in thirds(jnp.where(high >= 0, s, 0.0))] for s in stress]
        for sub in range(8):
            one = slice(sub, sub + 1)
            mask = iota((GROUPS, NZ), 0) == high[one]
            parts = [jnp.where(mask, pieces[c][k][one], 0.0) for k in range(3) for c in range(2)]
            a_slot[g, :, sub * NZ : (sub + 1) * NZ] = jnp.concatenate(parts, axis=0).astype(bf16)
        total = mm(a_slot[g], b_rows[pl.ds((g * 8 * NZ if isinstance(g, int) else pl.multiple_of(g * 8 * NZ, 8 * NZ)), 8 * NZ), :])
        width = 2 * GROUPS
        so_far[...] = so_far[...] + ((total[0:width] + total[width : 2 * width]) + total[2 * width : 3 * width])

    def by_cell(load):
        return jnp.transpose(jnp.concatenate([load, jnp.zeros((NZ - 2 * GROUPS, NZ), f32)], axis=0))

    def group(g, carry):
        lax.fori_loop(g * SIDE, (g + 1) * SIDE, arrived, 0)
        group_load(wall_stress(group_sums(0, g), group_sums(1, g), eight_rows(meta_rey, g)), g)
        return carry

    so_far[...] = jnp.zeros((2 * GROUPS, NZ), f32)
    lax.fori_loop(0, SIDE, group, 0)
    load = so_far[...]

    spread = by_cell(load)
    for c in range(2):
        for block in range(CELLS // NZ):
            at = pl.ds(c * SPAN + CY + block * NZ, NZ)
            column = c * GROUPS + block
            v1[at, :] = v1[at, :] - spread[:, column : column + 1] * profile

    edges(v1, None, ex2, ey2)
    halos2 = halo_copies(ex2, ey2, hx2, hy2, 4)
    for copy in halos2:
        copy.start()

    pieces = jnp.concatenate(thirds(load), axis=0)
    width = 2 * GROUPS
    so_far[...] = jnp.zeros((2 * GROUPS, NZ), f32)

    def second_group(g, carry):
        high = eight_rows(slot_hi, g)
        seen = mm(pieces, b_slot[:, pl.ds((g * 8 * NZ if isinstance(g, int) else pl.multiple_of(g * 8 * NZ, 8 * NZ)), 8 * NZ)])
        seen = (seen[0:width] + seen[width : 2 * width]) + seen[2 * width : 3 * width]
        met_load = [[], []]
        for sub in range(8):
            mask = iota((GROUPS, NZ), 0) == high[sub : sub + 1]
            for c in range(2):
                at_face = jnp.where(mask, seen[c * GROUPS : (c + 1) * GROUPS, sub * NZ : (sub + 1) * NZ], 0.0)
                met_load[c].append(jnp.sum(at_face, axis=0, keepdims=True))
        met_load = [jnp.concatenate(rows, axis=0) for rows in met_load]
        shape = group_sums(4, g)
        stress = wall_stress(
            group_sums(2, g) - met_load[0] * shape, group_sums(3, g) - met_load[1] * shape, eight_rows(meta_rey, g)
        )
        beside = pltpu.roll(stress[1], BLOCK, 1)
        for k in range(SIDE):
            rsend[g * SIDE + k] = jnp.where(lanes8 == k, stress[0], beside)
        return stress

    stresses = [second_group(g, 0) for g in range(SIDE)]
    for step in range(1, GROUPS):
        stress_copy(step).start()
    for g in range(SIDE):
        group_load(stresses[g], g)

    load = so_far[...]
    spread = by_cell(load)
    for c in range(2):
        for block in range(CELLS // NZ):
            at = pl.ds(c * SPAN + CY + block * NZ, NZ)
            column = c * GROUPS + block
            out[pl.ds(c * CELLS + block * NZ, NZ), :] = v1[at, :] - spread[:, column : column + 1] * profile

    lax.fori_loop(1, CX // RUN - 1, second_step, 0)
    for copy in halos:
        copy.wait_send()
    for step in range(1, GROUPS):
        meta_copy(step).wait_send()
        weight_copy(step).wait_send()
    for copy in halos2:
        copy.wait_recv()
    for c in range(2):
        v1[pl.ds(c * SPAN + (CX + 1) * CY, CY), :] = hx2[0, pl.ds(c * CY, CY), :]
        v1[pl.ds(c * SPAN, CY), :] = hx2[1, pl.ds(c * CY, CY), :]
    lax.fori_loop(0, 2, lambda n, carry: second_step(n * (CX // RUN - 1), carry), 0)
    for side, row, sign in ((0, CY - 1, 1.0), (1, 0, -1.0)):
        factor = factors[2 + side, pl.ds(row, CX, stride=CY), :]
        factor = factor + (sign * -0.5 * time_step) * v1[pl.ds(SPAN + CY + row, CX, stride=CY), :]
        for c in range(2):
            added = hy2[side, pl.ds(c * CX, CX), :] * factor
            most = CX - 8
            at = pl.ds(c * CELLS + row, most, stride=CY)
            out[at, :] = out[at, :] + added[:most]
            for x in range(most, CX):
                at = pl.ds(c * CELLS + row + x * CY, 1)
                out[at, :] = out[at, :] + added[x : x + 1]

    for step in range(1, GROUPS):
        stress_copy(step).wait_recv()
    back = jnp.concatenate([rows for g in range(SIDE) for rows in four(rsend[0], rrecv, g)], axis=0)
    pieces = jnp.concatenate(thirds(back), axis=0)
    width = SIDE * 16
    for ch in range(chunks):
        one = slice(ch, ch + 1)
        span = slice(ch * NZ, (ch + 1) * NZ)
        seen = b_face[:, span]
        spread = mm(pieces, seen)
        spread = (spread[0:width] + spread[width : 2 * width]) + spread[2 * width : 3 * width]
        place = hi_face[one, :]
        row = (place // 8) * 16 + place % 8
        for c in range(2):
            mask = iota((SIDE * 16, NZ), 0) == row + c * 8
            stress_out[c : c + 1, span] = jnp.sum(jnp.where(mask, spread, 0.0), axis=0, keepdims=True)

    for copy in halos2:
        copy.wait_send()
    for step in range(1, GROUPS):
        stress_copy(step).wait_send()


def write_out(velocity, stress, velocity_out, stress_out, sem):
    rows = 2 * CELLS // PIECES
    copies = [pltpu.make_async_copy(stress, stress_out, sem.at[PIECES])]
    for n in range(PIECES):
        part = pl.ds(n * rows, rows)
        copies.append(pltpu.make_async_copy(velocity.at[part], velocity_out.at[part], sem.at[n]))
    for copy in copies:
        copy.start()
    for copy in copies:
        copy.wait()


def local(velocity, metric, weights, reynolds, face_tile, face_cell, profile):
    vm = pltpu.VMEM
    dma = pltpu.SemaphoreType.DMA
    small = (FACES // NZ, NZ)
    scratch = [
        vm((2 * SPAN, NZ), f32), vm((2 * SPAN, NZ), f32), vm((SPAN, NZ), f32), vm((FACES, NZ), f32),
        vm((SLOTS, NZ), f32), vm((SLOTS, NZ), f32),
        vm((GROUPS, 8, NZ), f32), vm((GROUPS, 8, NZ), f32),
        vm(small, i32), vm(small, i32), vm((14 * GROUPS, FACES), bf16), vm((NZ, FACES), bf16),
        vm((2 * GROUPS, NZ), f32), vm((2 * GROUPS, NZ), f32),
        vm((2 * GROUPS, NZ), i32), pltpu.SMEM((2 * GROUPS, NZ), i32),
        vm((2 * GROUPS, NZ), i32), pltpu.SMEM((2 * GROUPS, NZ), i32),
        vm((4 * CELLS + 8, NZ), f32), vm((4 * CAP + 8, NZ), f32), vm((5 * GROUPS, 8, NZ), f32),
        vm((NZ, SLOTS), bf16), vm((SLOTS, NZ), bf16), vm((SIDE, 6 * GROUPS, 8 * NZ), bf16), vm((2 * GROUPS, NZ), f32),
        vm((6, CELLS + CY, NZ), f32), vm((2 * GROUPS, NZ), i32),
        vm((2, 3 * CY, NZ), f32), vm((2, 3 * CX, NZ), f32), vm((2, 2 * CY, NZ), f32), vm((2, 2 * CX, NZ), f32),
        vm((2, 3 * CY, NZ), f32), vm((2, 3 * CX, NZ), f32), vm((2, 2 * CY, NZ), f32), vm((2, 2 * CX, NZ), f32),
        vm((GROUPS, 8, NZ), f32), vm((GROUPS, 8, NZ), f32),
        vm(small, f32), vm(small, i32), vm(small, i32), vm((1, NZ), f32),
        dma((8,)), dma((2,)), dma((GROUPS,)), dma((GROUPS,)), dma((GROUPS,)), dma((GROUPS,)),
        dma((8,)), dma((8,)), dma((GROUPS,)), dma((GROUPS,)),
    ]
    whole = pl.BlockSpec(memory_space=pltpu.HBM)
    inside = pl.BlockSpec(memory_space=pltpu.VMEM)
    out, stress = pl.pallas_call(
        kernel,
        out_shape=(
            pltpu.VMEM((2 * CELLS, NZ), f32),
            pltpu.VMEM((2, FACES), f32),
        ),
        in_specs=[whole] * 7,
        out_specs=(inside, inside),
        scratch_shapes=scratch,
        compiler_params=pltpu.CompilerParams(
            collective_id=0, has_side_effects=True, vmem_limit_bytes=48 * 1024 * 1024
        ),
    )(*[pltpu.with_memory_space_constraint(array, pltpu.HBM) for array in (
        velocity.reshape(2 * CELLS, NZ), metric.reshape(CELLS, NZ), weights,
        reynolds.reshape(small), face_tile.reshape(small), face_cell.reshape(small), profile.reshape(1, NZ),
    )])
    out, stress = pl.pallas_call(
        write_out,
        out_shape=(
            jax.ShapeDtypeStruct((2 * CELLS, NZ), f32),
            jax.ShapeDtypeStruct((2, FACES), f32),
        ),
        in_specs=[inside, inside],
        out_specs=(whole, whole),
        scratch_shapes=[dma((PIECES + 1,))],
        compiler_params=pltpu.CompilerParams(vmem_limit_bytes=4 * 1024 * 1024),
    )(*[pltpu.with_memory_space_constraint(array, pltpu.VMEM) for array in (out, stress)])
    return out.reshape(2, CX, CY, NZ), stress


def solution(mesh):
    placed = (
        P(None, "gx", "gy", None),
        P("gx", "gy", None),
        P(("gx", "gy"), None),
        P(("gx", "gy")),
        P(("gx", "gy"), None),
        P(("gx", "gy")),
        P(),
    )
    return jax.shard_map(
        local,
        mesh=mesh,
        in_specs=placed,
        out_specs=(P(None, "gx", "gy", None), P(None, ("gx", "gy"))),
        check_vma=False,
    )
```
